32 devices in a mesh: patch: 2 (over x), sim: 16 (over z, y, core).
Axes of the slice: x: 2, y: 2, z: 4, core: 2. Of those that a mesh axis runs over, the one named last changes fastest.
Arguments:
- sky_maps: bfloat16 [2048, 2048], P(('patch', 'sim')), parts along dimension 0, may hold values from -6 to 6
- ivf_maps: bfloat16 [2048, 2048], P(('patch', 'sim')), parts along dimension 0, may hold values from -6 to 6
- sim_sky: bfloat16 [8, 2048, 2048], P(None, ('patch', 'sim')), parts along dimension 1, may hold values from -6 to 6
- sim_ivf: bfloat16 [8, 2048, 2048], P(None, ('patch', 'sim')), parts along dimension 1, may hold values from -6 to 6
- ra_wiener: bfloat16 [1024, 1024], replicated, may hold values from -0.1875 to 0.1875
- ra_gradient: bfloat16 [1024, 1024], replicated, may hold values from -0.1875 to 0.1875
- pair_table: int32 [8, 8], replicated, may hold values 0 or 1
- sim_index: int32 [4], replicated, may hold values from 0 to 7
- source_pixels: int32 [8192], P('patch'), parts along dimension 0, may hold values from 0 to 262143
- response: float32 [256], P('patch'), parts along dimension 0, may hold values from 0.2 to 2
Outputs:
- lens_split: float32 [2048, 2048], P(('patch', 'sim')), parts along dimension 0
The draws below stay inside these ranges and needn't reach their ends.
There are 2 independent parts, one for each index of `patch`. The reference program is written for one: setup_inputs(seed, part) draws one part's arguments, and reference() takes and returns one part's arrays. A program takes and returns all parts, laid end to end along the dimension named above; an argument that names none is the same for every part. Nothing has to cross between parts.
Inputs may be any that keep to these rules, and one draw needn't show every extreme that they name: `sim_index`: indices into the cached evolutions; entries may repeat. `source_pixels`: flat pixel indices of the patch; entries may repeat.
All inputs are finite; a program needn't handle non-finite values.
Results may differ from the reference program's by a relative error of at most 0.0035.
Values may be sent and summed in bfloat16 or wider, within the bound.
No kernel may reach another device: no remote copies, remote signals or barrier semaphores. Data moves between devices by JAX's collectives and lax.ppermute only.
A program may use at most 128 MiB of HBM per device.

```python
import math
import jax
import jax.numpy as jnp
from jax import lax

NSPLIT = 8
ROWS_DEV = 64
COLS = 2048
FT = 1024
SIM_CACHE = 8
NUSE = 4
NSRC = 4096
NB = 2
NROWS = 128
SROWS = 1024


def set_ends(entries, stream_key, smallest, top_value):
    spot = [jax.random.randint(jax.random.fold_in(stream_key, axis), (), 0, length) for axis, length in enumerate(entries.shape)]
    widest = entries.shape.index(max(entries.shape))
    beside = spot[:widest] + [(spot[widest] + 1) % entries.shape[widest]] + spot[widest + 1:]
    return entries.at[tuple(spot)].set(smallest).at[tuple(beside)].set(top_value)


def block_levels(own_key, dims, pieces, least, high):
    level, own = 1.0, jax.random.fold_in(own_key, 6)
    for position, parts in pieces:
        draws = jnp.exp(jax.random.uniform(jax.random.fold_in(own, position), (parts,), jnp.float32, least / len(pieces), high / len(pieces)))
        level = level * jnp.repeat(draws, dims[position] // parts).reshape([-1 if axis == position else 1 for axis in range(len(dims))])
    return level


def centred(own_key, dims, scale, bound, shards=(), held_as=jnp.bfloat16):
    factor_of = block_levels(own_key, dims, shards, -0.22, 0.18) if shards else 1.0
    entries = jax.random.normal(own_key, dims, jnp.float32) * scale * factor_of
    return jnp.minimum(jnp.maximum(entries, -bound), bound).astype(held_as)


def setup_inputs(seed: int = 0, part: int = 0) -> dict:
    splits = jax.random.split(jax.random.key(seed), 11)
    own_keys = jax.random.split(jax.random.fold_in(splits[10], part), 11)
    sky_maps = centred(own_keys[0], (SROWS, COLS), 1.0, 6.0, ((0, 16),))
    ivf_maps = centred(own_keys[1], (SROWS, COLS), 1.0, 6.0, ((0, 16),))
    sim_sky = centred(own_keys[2], (SIM_CACHE, SROWS, COLS), 1.0, 6.0, ((1, 16),))
    sim_ivf = centred(own_keys[3], (SIM_CACHE, SROWS, COLS), 1.0, 6.0, ((1, 16),))
    ra_wiener = centred(splits[4], (FT, FT), FT ** -0.5, 0.1875)
    ra_gradient = centred(splits[5], (FT, FT), FT ** -0.5, 0.1875)
    pair_table = set_ends((jax.random.randint(splits[6], (NSPLIT, NSPLIT), 0, 4) < 3).astype(jnp.int32), jax.random.fold_in(splits[6], 1), 0, 1)
    sim_index = set_ends(jax.random.randint(splits[7], (NUSE,), 0, SIM_CACHE), jax.random.fold_in(splits[7], 1), 0, SIM_CACHE - 1).astype(jnp.int32)
    source_pixels = set_ends(jax.random.randint(own_keys[8], (NSRC,), 0, NROWS * COLS), jax.random.fold_in(own_keys[8], 1), 0, (NROWS * COLS) - 1).astype(jnp.int32)
    response = jnp.clip(jnp.exp(jax.random.uniform(own_keys[9], (NROWS,), jnp.float32, math.log(0.2), math.log(2.0))), 0.2, 2.0)
    return {"sky_maps": sky_maps, "ivf_maps": ivf_maps, "sim_sky": sim_sky, "sim_ivf": sim_ivf, "ra_wiener": ra_wiener, "ra_gradient": ra_gradient, "pair_table": pair_table, "sim_index": sim_index, "source_pixels": source_pixels, "response": response}


def tile_apply(values, matrix):
    width = matrix.shape[0]
    shaped = values.reshape(values.shape[:-1] + (values.shape[-1] // width, width)).astype(jnp.float32)
    result = jnp.einsum("...tc,cd->...td", shaped, matrix.astype(jnp.float32))
    return result.reshape(values.shape)


def row_slope(values):
    padded = jnp.pad(values.astype(jnp.float32), ((0, 0), (1, 1), (0, 0)))
    return (padded[:, 2:] - padded[:, :-2]) * 0.5


def estimate(sky, ivf, keep, pair_weights, ra_wiener, ra_gradient, response):
    masked = ivf * keep[None]
    wiener = tile_apply(sky, ra_wiener).astype(jnp.bfloat16)
    grad_ra = tile_apply(masked, ra_gradient)
    grad_dec = row_slope(masked)
    sum_ra = jnp.einsum("sj,jrc->src", pair_weights, grad_ra)
    sum_dec = jnp.einsum("sj,jrc->src", pair_weights, grad_dec)
    sum_src = jnp.einsum("sj,jrc->src", pair_weights, masked.astype(jnp.float32))
    wiener_wide = wiener.astype(jnp.float32)
    flux_ra = (wiener_wide * sum_ra).astype(jnp.bfloat16)
    flux_dec = wiener_wide * sum_dec
    divergence = tile_apply(flux_ra, ra_gradient) + row_slope(flux_dec)
    return -divergence - response[None, :, None] * (wiener_wide * sum_src)


def reference(sky_maps, ivf_maps, sim_sky, sim_ivf, ra_wiener, ra_gradient, pair_table, sim_index, source_pixels, response):
    offset_rows = (NB // 2) * ROWS_DEV
    hit = jnp.zeros((NROWS * COLS,), jnp.bfloat16).at[source_pixels].set(1)
    keep = (1 - hit).reshape(NROWS, COLS)
    others = 1.0 - jnp.eye(NSPLIT, dtype=jnp.float32)
    pair_weights = pair_table.astype(jnp.float32) * others
    shape3 = (NSPLIT, NROWS, COLS)

    def ordered(values):
        return jnp.roll(values, -offset_rows, axis=0).reshape(shape3)

    data_part = estimate(ordered(sky_maps), ordered(ivf_maps), keep, pair_weights, ra_wiener, ra_gradient, response)
    mean_field = jnp.zeros(shape3, jnp.float32)
    for member in range(NUSE):
        chosen = sim_index[member]
        sky_one = ordered(lax.dynamic_index_in_dim(sim_sky, chosen, 0, keepdims=False))
        ivf_one = ordered(lax.dynamic_index_in_dim(sim_ivf, chosen, 0, keepdims=False))
        mean_field = mean_field + estimate(sky_one, ivf_one, keep, pair_weights, ra_wiener, ra_gradient, response)
    result = data_part - mean_field / NUSE
    return jnp.roll(result.reshape(SROWS, COLS), offset_rows, axis=0)
```

```python
import functools

import jax
import jax.numpy as jnp
from jax import lax
from jax.experimental import pallas as pl
from jax.experimental.pallas import tpu as pltpu
from jax.sharding import PartitionSpec as P

GROUPS = ((0, 1, 2), (3, 4))
PIXEL_CHUNK = 1024
LOW_COLUMNS = 256
VMEM_LIMIT = 40 * 1024 * 1024

F32 = jnp.float32
BF16 = jnp.bfloat16
SMEM = pl.BlockSpec(memory_space=pltpu.SMEM)
VMEM = pl.BlockSpec(memory_space=pltpu.VMEM)
ANY = pl.BlockSpec(memory_space=pl.ANY)
PARAMS = pltpu.CompilerParams(vmem_limit_bytes=VMEM_LIMIT)


def cost(flops, bytes_accessed):
    return pl.CostEstimate(flops=int(flops), bytes_accessed=int(bytes_accessed), transcendentals=0)


def send_order(count):
    return list(range(count - 1, -1, -1))


def keep_kernel(rows, width, a_ref, b_ref, keep_ref, total):
    pixels = a_ref.shape[1]
    tall = total.shape[0]
    total[...] = jnp.zeros_like(total)

    @pl.loop(0, pixels // PIXEL_CHUNK)
    def _(step):
        part = pl.ds(pl.multiple_of(step * PIXEL_CHUNK, PIXEL_CHUNK), PIXEL_CHUNK)
        high = lax.broadcasted_iota(jnp.int32, (tall, PIXEL_CHUNK), 0) == a_ref[:, part]
        low = lax.broadcasted_iota(jnp.int32, (LOW_COLUMNS, PIXEL_CHUNK), 0) == b_ref[:, part]
        total[...] += lax.dot_general(
            high.astype(F32).astype(BF16),
            low.astype(F32).astype(BF16),
            (((1,), (1,)), ((), ())),
            preferred_element_type=F32,
        )

    per_tile = width // LOW_COLUMNS
    for block in range(tall // rows):
        tile, piece = block // per_tile, block % per_tile
        count = total[block * rows : (block + 1) * rows, :]
        keep_ref[tile, :, piece * LOW_COLUMNS : (piece + 1) * LOW_COLUMNS] = jnp.where(
            count > 0, 0.0, 1.0
        ).astype(BF16)


def keep_mask(source_pixels, band_index, rows, columns, width):
    offsets = source_pixels - band_index * rows * columns
    inside = (offsets >= 0) & (offsets < rows * columns)
    row, column = offsets // columns, offsets % columns
    a = jnp.where(inside, (column // LOW_COLUMNS) * rows + row, -1)
    b = column % LOW_COLUMNS
    pixels = source_pixels.shape[0]
    extra = -pixels % PIXEL_CHUNK
    a = jnp.pad(a, (0, extra), constant_values=-1)[None]
    b = jnp.pad(b, (0, extra))[None]
    tall = columns // LOW_COLUMNS * rows
    return pl.pallas_call(
        functools.partial(keep_kernel, rows, width),
        out_shape=jax.ShapeDtypeStruct((columns // width, rows, width), BF16),
        in_specs=[VMEM, VMEM],
        out_specs=VMEM,
        scratch_shapes=[pltpu.VMEM((tall, LOW_COLUMNS), F32)],
        compiler_params=PARAMS,
        cost_estimate=cost(2 * tall * LOW_COLUMNS * (pixels + extra), 4 * rows * columns),
        name="keep",
    )(a, b)


def wiener_kernel(index_ref, first_ref, sky_ref, sim_ref, matrix_ref, out_ref, head_ref, tail_ref, edge_ref):
    field = pl.program_id(0)
    tiles, rows, width = out_ref.shape[1:]

    def apply(source):
        for tile in range(tiles):
            values = source(pl.ds(tile * width, width))
            result = jnp.dot(values, matrix_ref[...], preferred_element_type=F32).astype(BF16)
            out_ref[0, tile] = result
            head = result[:1].astype(F32)
            tail = result[rows - 1 :].astype(F32)
            head_ref[0, tile] = head.astype(BF16)
            tail_ref[0, tile] = tail.astype(BF16)
            edge_ref[0, tile] = jnp.where(first_ref[0] > 0, tail, head).astype(BF16)

    @pl.when(field == 0)
    def _():
        apply(lambda part: sky_ref[:, part])

    @pl.when(field > 0)
    def _():
        apply(lambda part: sim_ref[0, :, part])


def wiener_fields(sim_index, first, sky_maps, sim_sky, matrix):
    rows, columns = sky_maps.shape
    width = matrix.shape[0]
    tiles = columns // width
    fields = sim_index.shape[0] + 1
    own = jnp.concatenate([sim_index[:1], sim_index])
    edge_shape = jax.ShapeDtypeStruct((fields, tiles, 1, width), BF16)
    edge_spec = pl.BlockSpec((1, tiles, 1, width), lambda f, *_: (f, 0, 0, 0))
    return pl.pallas_call(
        wiener_kernel,
        out_shape=[jax.ShapeDtypeStruct((fields, tiles, rows, width), BF16)] + [edge_shape] * 3,
        grid_spec=pltpu.PrefetchScalarGridSpec(
            num_scalar_prefetch=2,
            grid=(fields,),
            in_specs=[
                pl.BlockSpec((rows, columns), lambda f, *_: (0, 0)),
                pl.BlockSpec((1, rows, columns), lambda f, index, *_: (index[f], 0, 0)),
                pl.BlockSpec((width, width), lambda f, *_: (0, 0)),
            ],
            out_specs=[
                pl.BlockSpec((1, tiles, rows, width), lambda f, *_: (f, 0, 0, 0))
            ] + [edge_spec] * 3,
        ),
        compiler_params=PARAMS,
        cost_estimate=cost(2 * fields * rows * columns * width, 4 * fields * rows * columns),
        name="wiener",
    )(own, first, sky_maps, sim_sky, matrix)


def pack_kernel(group, parts, index_ref, row_ref, column_ref, ivf_ref, sim_ref, *refs):
    outs, sems = refs[:parts], refs[parts]
    depth, width = outs[0].shape[1:]
    copies = []
    for d in send_order(parts):
        part = (
            pl.ds(pl.multiple_of(row_ref[d], depth), depth),
            pl.ds(pl.multiple_of(column_ref[d], width), width),
        )
        for place, field in enumerate(group):
            source = ivf_ref.at[part] if field == 0 else sim_ref.at[(index_ref[field - 1],) + part]
            copy = pltpu.make_async_copy(source, outs[d].at[place], sems.at[d, place])
            copy.start()
            copies.append(copy)
    for copy in copies:
        copy.wait()


def pack(group, sim_index, slot_rows, slot_columns, ivf_maps, sim_ivf, depth, width):
    parts = slot_rows.shape[0]
    shape = jax.ShapeDtypeStruct((len(group), depth, width), BF16)
    return pl.pallas_call(
        functools.partial(pack_kernel, group, parts),
        out_shape=[shape] * parts,
        in_specs=[SMEM, SMEM, SMEM, ANY, ANY],
        out_specs=[ANY] * parts,
        scratch_shapes=[pltpu.SemaphoreType.DMA((parts, len(group)))],
        compiler_params=PARAMS,
        cost_estimate=cost(0, 4 * parts * len(group) * depth * width),
        name="pack",
    )(sim_index, slot_rows, slot_columns, ivf_maps, sim_ivf)


def mix_kernel(parts, weights_ref, *refs):
    chunks, outs = refs[:parts], refs[parts:]
    fields, depth, _ = chunks[0].shape
    for place in range(fields):
        stacked = jnp.concatenate([chunk[place] for chunk in chunks], axis=0)
        mixed = jnp.dot(weights_ref[...], stacked, preferred_element_type=F32).astype(BF16)
        for d in range(parts):
            outs[d][place] = mixed[d * depth : (d + 1) * depth]


def mix(weights, chunks):
    parts = len(chunks)
    shape = chunks[0].shape
    size = shape[0] * shape[1] * shape[2]
    return pl.pallas_call(
        functools.partial(mix_kernel, parts),
        out_shape=[jax.ShapeDtypeStruct(shape, BF16)] * parts,
        in_specs=[VMEM] * (parts + 1),
        out_specs=[VMEM] * parts,
        compiler_params=PARAMS,
        cost_estimate=cost(2 * parts * size * weights.shape[0], 4 * parts * size),
        name="mix",
    )(weights, *chunks)


def assemble_kernel(parts, first_ref, row_ref, tile_ref, keep_ref, *refs):
    chunks = refs[:parts]
    out_ref, head_ref, tail_ref, edge_ref = refs[parts:]
    fields, _, rows, _ = out_ref.shape
    depth = chunks[0].shape[1]
    for d in range(parts):
        part = pl.ds(pl.multiple_of(row_ref[d], depth), depth)
        tile = tile_ref[d]
        keep = keep_ref[tile, part, :]
        for place in range(fields):
            out_ref[place, tile, part, :] = chunks[d][place] * keep
    for place in range(fields):
        for tile in range(out_ref.shape[1]):
            head = out_ref[place, tile, 0:16, :].astype(F32)[:2]
            tail = out_ref[place, tile, rows - 16 : rows, :].astype(F32)[14:]
            head_ref[place, tile] = head.astype(BF16)
            tail_ref[place, tile] = tail.astype(BF16)
            edge_ref[place, tile] = jnp.where(first_ref[0] > 0, tail, head).astype(BF16)


def assemble(first, slot_rows, slot_tiles, keep, chunks):
    parts = len(chunks)
    fields, depth, width = chunks[0].shape
    tiles, rows, _ = keep.shape
    edge_shape = jax.ShapeDtypeStruct((fields, tiles, 2, width), BF16)
    return pl.pallas_call(
        functools.partial(assemble_kernel, parts),
        out_shape=[jax.ShapeDtypeStruct((fields, tiles, rows, width), BF16)] + [edge_shape] * 3,
        in_specs=[SMEM] * 3 + [VMEM] * (parts + 1),
        out_specs=[VMEM] * 4,
        compiler_params=PARAMS,
        cost_estimate=cost(fields * tiles * rows * width, 4 * fields * tiles * rows * width),
        name="assemble",
    )(first, slot_rows, slot_tiles, keep, *chunks)


def slope(values):
    rows = values.shape[0]
    line = lax.broadcasted_iota(jnp.int32, values.shape, 0)
    above = jnp.where(line == rows - 1, 0.0, pltpu.roll(values, rows - 1, 0))
    below = jnp.where(line == 0, 0.0, pltpu.roll(values, 1, 0))
    return (above - below) * 0.5


def home_kernel(group, uses, earlier, final, *refs):
    refs = list(refs)
    sums_ref, wiener_ref, matrix_ref = refs[:3]
    before = refs[3 : 3 + 3 * earlier]
    rest = refs[3 + 3 * earlier :]
    fields, tiles, rows, width = sums_ref.shape
    totals = []
    for tile in range(tiles):
        ra = dec = src = None
        for place, field in enumerate(group):
            share = 1.0 if field == 0 else -1.0 / uses
            sums = sums_ref[place, tile]
            grad = jnp.dot(sums, matrix_ref[...], preferred_element_type=F32)
            wide = sums.astype(F32)
            weight = wiener_ref[field, tile].astype(F32) * share
            terms = weight * grad, weight * slope(wide), weight * wide
            if ra is None:
                ra, dec, src = terms
            else:
                ra, dec, src = ra + terms[0], dec + terms[1], src + terms[2]
        if earlier:
            ra, dec, src = ra + before[0][tile], dec + before[1][tile], src + before[2][tile]
        if not final:
            rest[0][tile], rest[1][tile], rest[2][tile] = ra, dec, src
        else:
            response_ref, out_ref = rest
            high = ra.astype(BF16)
            low = (ra - high.astype(F32)).astype(BF16)
            both = jnp.dot(
                jnp.concatenate([high, low], axis=0), matrix_ref[...], preferred_element_type=F32
            )
            divergence = both[:rows] + both[rows:] + slope(dec)
            out_ref[:, tile * width : (tile + 1) * width] = -divergence - response_ref[...] * src


def home(group, uses, sums, wiener, matrix, before, response, final):
    fields, tiles, rows, width = sums.shape
    shape = jax.ShapeDtypeStruct((tiles, rows, width), F32)
    out_shape = jax.ShapeDtypeStruct((rows, tiles * width), F32) if final else [shape] * 3
    operands = [sums, wiener, matrix, *before] + ([response] if final else [])
    return pl.pallas_call(
        functools.partial(home_kernel, group, uses, bool(before), final),
        out_shape=out_shape,
        in_specs=[VMEM] * len(operands),
        out_specs=VMEM if final else [VMEM] * 3,
        compiler_params=PARAMS,
        cost_estimate=cost(
            2 * (fields + 2 * final) * tiles * rows * width * width, 16 * tiles * rows * width
        ),
        name="home",
    )(*operands)


def rim_kernel(groups, uses, flags_ref, out_in_ref, w_head, w_tail, w_lo, w_hi, *refs):
    out_ref = refs[-1]
    tiles, width = w_head.shape[1], w_head.shape[3]
    side = pl.program_id(0)
    out_ref[...] = out_in_ref[...]

    def terms(own_w, far_w, pick):
        for tile in range(tiles):
            inner = outer = 0.0
            for number, group in enumerate(groups):
                s_head, s_tail, s_lo, s_hi = refs[4 * number : 4 * number + 4]
                for place, field in enumerate(group):
                    share = (1.0 if field == 0 else -1.0 / uses) * 0.25
                    near, beyond, own = pick(s_head, s_tail, s_lo, s_hi, place, tile)
                    inner += own_w[field, tile].astype(F32) * near * share
                    outer += far_w[field, tile].astype(F32) * (own - beyond) * share
            yield pl.ds(tile * width, width), inner, outer

    @pl.when((side == 0) & (flags_ref[0] > 0))
    def _():
        def pick(s_head, s_tail, s_lo, s_hi, place, tile):
            far = s_lo[place, tile].astype(F32)
            return far[1:2], far[0:1], s_head[place, tile].astype(F32)[0:1]

        for part, inner, outer in terms(w_head, w_lo, pick):
            out_ref[1:2, part] = out_ref[1:2, part] - inner
            out_ref[0:1, part] = out_ref[0:1, part] + outer

    @pl.when((side == 1) & (flags_ref[1] > 0))
    def _():
        def pick(s_head, s_tail, s_lo, s_hi, place, tile):
            far = s_hi[place, tile].astype(F32)
            return far[0:1], far[1:2], s_tail[place, tile].astype(F32)[1:2]

        last = out_ref.shape[0] - 1
        for part, inner, outer in terms(w_tail, w_hi, pick):
            out_ref[last - 1 : last, part] = out_ref[last - 1 : last, part] - inner
            out_ref[last : last + 1, part] = out_ref[last : last + 1, part] + outer


def rim(groups, uses, flags, out, wiener_rims, sum_rims):
    rows, columns = out.shape
    block = pl.BlockSpec((8, columns), lambda side: (side * (rows // 8 - 1), 0))
    small = [*wiener_rims] + [array for rims in sum_rims for array in rims]

    def whole(array):
        zeros = (0,) * array.ndim
        return pl.BlockSpec(array.shape, lambda side: zeros)

    return pl.pallas_call(
        functools.partial(rim_kernel, groups, uses),
        out_shape=jax.ShapeDtypeStruct(out.shape, out.dtype),
        grid=(2,),
        in_specs=[SMEM, block] + [whole(array) for array in small],
        out_specs=block,
        input_output_aliases={1: 0},
        compiler_params=PARAMS,
        cost_estimate=cost(0, 64 * columns),
        name="rim",
    )(flags, out, *small)


def on_device(
    sky_maps,
    ivf_maps,
    sim_sky,
    sim_ivf,
    ra_wiener,
    ra_gradient,
    pair_table,
    sim_index,
    source_pixels,
    response,
):
    splits = pair_table.shape[0]
    uses = sim_index.shape[0]
    axis_count = lax.axis_size("sim")
    bands = axis_count // splits
    device = lax.axis_index("sim")
    logical = (device - bands // 2) % axis_count
    band = logical % bands
    rows, columns = sky_maps.shape
    width = ra_gradient.shape[0]
    tiles = columns // width
    depth = rows * tiles // splits

    place, lane = device // bands, device % bands
    slots = place ^ jnp.arange(splits)
    slot_rows = (slots // tiles * depth).astype(jnp.int32)
    slot_tiles = (slots % tiles).astype(jnp.int32)
    slot_columns = slot_tiles * width

    def swap(block, d):
        if d == 0:
            return block
        pairs = [
            (g * bands + u, (g ^ d) * bands + u) for g in range(splits) for u in range(bands)
        ]
        return lax.ppermute(block, "sim", pairs)

    def exchange(blocks):
        moved = {d: swap(blocks[d], d) for d in send_order(splits)}
        return [moved[d] for d in range(splits)]

    def neighbours(head, tail, edge):
        if bands == 2:
            pairs = [((k + 1) % axis_count, k) if (k - 1) % 2 == 0 else ((k - 1) % axis_count, k)
                     for k in range(axis_count)]
            got = lax.ppermute(edge, "sim", pairs)
            return got, got
        ahead = [(k, (k + 1) % axis_count) for k in range(axis_count)]
        back = [((k + 1) % axis_count, k) for k in range(axis_count)]
        return lax.ppermute(tail, "sim", ahead), lax.ppermute(head, "sim", back)

    first = (band == 0).astype(jnp.int32)[None]
    flags = jnp.stack([band > 0, band < bands - 1]).astype(jnp.int32)

    split_of = (slots - (lane < bands // 2)) % splits
    pairs = jnp.where(split_of[:, None] == split_of[None], 0, pair_table[split_of][:, split_of])
    weights = jnp.kron(pairs.astype(F32), jnp.eye(depth, dtype=F32)).astype(BF16)

    sent = [
        pack(group, sim_index, slot_rows, slot_columns, ivf_maps, sim_ivf, depth, width)
        for group in GROUPS
    ]
    arrived = [exchange(blocks) for blocks in sent]
    keep = keep_mask(source_pixels, band, rows, columns, width)
    wiener, *w_edges = wiener_fields(sim_index, first, sky_maps, sim_sky, ra_wiener)
    w_lo, w_hi = neighbours(*w_edges)
    returned = [exchange(mix(weights, blocks)) for blocks in arrived]
    band_response = lax.dynamic_slice_in_dim(response, band * rows, rows)[:, None]
    before, sum_rims = [], []
    for number, group in enumerate(GROUPS):
        sums, *edges = assemble(first, slot_rows, slot_tiles, keep, returned[number])
        s_lo, s_hi = neighbours(*edges)
        sum_rims.append([edges[0], edges[1], s_lo, s_hi])
        final = number == len(GROUPS) - 1
        before = home(group, uses, sums, wiener, ra_gradient, before, band_response, final)
    return rim(GROUPS, uses, flags, before, [w_edges[0], w_edges[1], w_lo, w_hi], sum_rims)


def solution(mesh):
    in_specs = (
        P(("patch", "sim"), None),
        P(("patch", "sim"), None),
        P(None, ("patch", "sim"), None),
        P(None, ("patch", "sim"), None),
        P(),
        P(),
        P(),
        P(),
        P("patch"),
        P("patch"),
    )
    out_specs = P(("patch", "sim"), None)
    return jax.shard_map(
        on_device, mesh=mesh, in_specs=in_specs, out_specs=out_specs, check_vma=False
    )
```

```python
import functools

import jax
import jax.numpy as jnp
from jax import lax
from jax.experimental import pallas as pl
from jax.experimental.pallas import tpu as pltpu
from jax.sharding import PartitionSpec as P

PIXEL_CHUNK = 1024
LOW_COLUMNS = 256
MIB = 1024 * 1024

F32 = jnp.float32
BF16 = jnp.bfloat16
SMEM = pl.BlockSpec(memory_space=pltpu.SMEM)
VMEM = pl.BlockSpec(memory_space=pltpu.VMEM)
ANY = pl.BlockSpec(memory_space=pl.ANY)
WIDE_PARAMS = pltpu.CompilerParams(vmem_limit_bytes=60 * MIB)
PARAMS = pltpu.CompilerParams(vmem_limit_bytes=24 * MIB)

EARLY = (1, 7, 6)
LATE = (2, 3, 5, 4)


def cost(flops, bytes_accessed):
    return pl.CostEstimate(flops=int(flops), bytes_accessed=int(bytes_accessed), transcendentals=0)


def place_and_band(splits):
    count = lax.axis_size("sim")
    bands = count // splits
    device = lax.axis_index("sim")
    logical = lax.rem(device + (count - bands // 2), count)
    return lax.div(device, bands), lax.rem(logical, bands)


def slot_at(place, d, tiles, depth):
    slot = lax.bitwise_xor(place, d)
    block = lax.div(slot, tiles)
    half = lax.bitwise_and(lax.bitwise_xor(block, lax.div(block, 2)), 1)
    return half, pl.multiple_of(lax.div(block, 2) * depth, depth), lax.rem(slot, tiles)


def keep_kernel(rows, width, a_ref, b_ref, *refs):
    keep_ref, total = refs[-2:]
    pixels = a_ref.shape[1]
    tall = total.shape[0]
    total[...] = jnp.zeros_like(total)

    @pl.loop(0, pixels // PIXEL_CHUNK)
    def _(step):
        part = pl.ds(pl.multiple_of(step * PIXEL_CHUNK, PIXEL_CHUNK), PIXEL_CHUNK)
        high = lax.broadcasted_iota(jnp.int32, (tall, PIXEL_CHUNK), 0) == a_ref[:, part]
        low = lax.broadcasted_iota(jnp.int32, (LOW_COLUMNS, PIXEL_CHUNK), 0) == b_ref[:, part]
        total[...] += lax.dot_general(
            high.astype(F32).astype(BF16),
            low.astype(F32).astype(BF16),
            (((1,), (1,)), ((), ())),
            preferred_element_type=F32,
        )

    per_tile = width // LOW_COLUMNS
    for block in range(tall // rows):
        tile, piece = block // per_tile, block % per_tile
        count = total[block * rows : (block + 1) * rows, :]
        keep_ref[tile, :, piece * LOW_COLUMNS : (piece + 1) * LOW_COLUMNS] = jnp.where(
            count > 0, 0.0, 1.0
        ).astype(BF16)


def keep_mask(source_pixels, band_index, rows, columns, width, after):
    offsets = source_pixels - band_index * rows * columns
    inside = (offsets >= 0) & (offsets < rows * columns)
    row, column = offsets // columns, offsets % columns
    a = jnp.where(inside, (column // LOW_COLUMNS) * rows + row, -1)
    b = column % LOW_COLUMNS
    pixels = source_pixels.shape[0]
    extra = -pixels % PIXEL_CHUNK
    a = jnp.pad(a, (0, extra), constant_values=-1)[None]
    b = jnp.pad(b, (0, extra))[None]
    tall = columns // LOW_COLUMNS * rows
    return pl.pallas_call(
        functools.partial(keep_kernel, rows, width),
        out_shape=jax.ShapeDtypeStruct((columns // width, rows, width), BF16),
        in_specs=[VMEM, VMEM] + [ANY] * len(after),
        out_specs=VMEM,
        scratch_shapes=[pltpu.VMEM((tall, LOW_COLUMNS), F32)],
        compiler_params=PARAMS,
        cost_estimate=cost(2 * tall * LOW_COLUMNS * (pixels + extra), 4 * rows * columns),
        name="keep",
    )(a, b, *after)


def wiener_kernel(index_ref, sky_ref, sim_ref, matrix_ref, *refs):
    out_ref, held, sems = refs[-3:]
    fields, tiles, rows, width = out_ref.shape
    copies = [pltpu.make_async_copy(sky_ref, held.at[0], sems.at[0])]
    for field in range(1, fields):
        source = sim_ref.at[index_ref[field - 1]]
        copies.append(pltpu.make_async_copy(source, held.at[field], sems.at[field]))
    for copy in copies:
        copy.start()
    for copy in copies:
        copy.wait()
    for tile in range(tiles):
        values = held[:, :, tile * width : (tile + 1) * width].reshape(fields * rows, width)
        result = jnp.dot(values, matrix_ref[...], preferred_element_type=F32).astype(BF16)
        out_ref[:, tile] = result.reshape(fields, rows, width)


def wiener_fields(sim_index, sky_maps, sim_sky, matrix, after):
    rows, columns = sky_maps.shape
    width = matrix.shape[0]
    fields = sim_index.shape[0] + 1
    return pl.pallas_call(
        wiener_kernel,
        out_shape=jax.ShapeDtypeStruct((fields, columns // width, rows, width), BF16),
        in_specs=[SMEM, ANY, ANY, VMEM] + [ANY] * len(after),
        out_specs=VMEM,
        scratch_shapes=[
            pltpu.VMEM((fields, rows, columns), BF16),
            pltpu.SemaphoreType.DMA((fields,)),
        ],
        compiler_params=PARAMS,
        cost_estimate=cost(2 * fields * rows * columns * width, 4 * fields * rows * columns),
        name="wiener",
    )(sim_index, sky_maps, sim_sky, matrix, *after)


def pack_kernel(order, index_ref, ivf_ref, sim_ref, *refs):
    outs, held, sems = refs[: len(order)], refs[-2], refs[-1]
    fields, depth, width = outs[0].shape
    rows, columns = ivf_ref.shape
    place, _ = place_and_band(len(order))
    copies = [pltpu.make_async_copy(ivf_ref, held.at[0], sems.at[0])]
    for field in range(1, fields):
        source = sim_ref.at[index_ref[field - 1]]
        copies.append(pltpu.make_async_copy(source, held.at[field], sems.at[field]))
    for copy in copies:
        copy.start()
    for field in range(fields):
        copies[field].wait()
        for d in order:
            half, row, tile = slot_at(place, d, columns // width, depth)
            part = pl.ds(pl.multiple_of(half * (rows // 2) + row, depth), depth)
            across = pl.ds(pl.multiple_of(tile * width, width), width)
            outs[d][field] = held[field, part, across]


def pack(splits, sim_index, ivf_maps, sim_ivf, depth, width):
    fields = sim_index.shape[0] + 1
    return pl.pallas_call(
        functools.partial(pack_kernel, range(splits)),
        out_shape=[jax.ShapeDtypeStruct((fields, depth, width), BF16)] * splits,
        in_specs=[SMEM, ANY, ANY],
        out_specs=[VMEM] * splits,
        scratch_shapes=[
            pltpu.VMEM((fields,) + ivf_maps.shape, BF16),
            pltpu.SemaphoreType.DMA((fields,)),
        ],
        compiler_params=WIDE_PARAMS,
        cost_estimate=cost(0, 4 * splits * fields * depth * width),
        name="pack",
    )(sim_index, ivf_maps, sim_ivf)


def mix_kernel(order, weights_ref, *refs):
    parts = len(order)
    chunks, outs = refs[:parts], refs[-parts:]
    fields, depth, _ = chunks[0].shape
    for field in range(fields):
        stacked = jnp.concatenate([chunks[order.index(d)][field] for d in range(parts)], axis=0)
        mixed = jnp.dot(weights_ref[...], stacked, preferred_element_type=F32).astype(BF16)
        for d in range(parts):
            outs[d][field] = mixed[d * depth : (d + 1) * depth]


def mix(weights, chunks, after):
    order = EARLY + LATE + (0,)
    parts = len(chunks)
    shape = chunks[0].shape
    size = shape[0] * shape[1] * shape[2]
    return pl.pallas_call(
        functools.partial(mix_kernel, order),
        out_shape=[jax.ShapeDtypeStruct(shape, BF16)] * parts,
        in_specs=[VMEM] * (parts + 1) + [ANY] * len(after),
        out_specs=[VMEM] * parts,
        compiler_params=PARAMS,
        cost_estimate=cost(2 * parts * size * weights.shape[0], 4 * parts * size),
        name="mix",
    )(weights, *[chunks[d] for d in order], *after)


def half_kernel(splits, order, late, share_ref, keep_ref, wiener_ref, matrix_ref, response_ref, *refs):
    chunks = refs[: len(order)]
    fields, depth, width = chunks[0].shape
    if late:
        early_sums_ref, early_part_ref, early_dec_ref = refs[len(order) : len(order) + 3]
        out_ref, sums_ref, dec_ref, grad_ref, ra_ref = refs[len(order) + 3 :]
    else:
        sums_ref, part_ref, early_dec_ref, grad_ref, ra_ref = refs[len(order) :]
    tiles, rows = sums_ref.shape[1:3]
    place, band = place_and_band(splits)
    half = slot_at(place, order[0], tiles, depth)[0]
    here = pl.ds(pl.multiple_of(half * rows, rows), rows)
    other = pl.ds(pl.multiple_of((1 - half) * rows, rows), rows)
    for d, chunk in zip(order, chunks):
        _, row, tile = slot_at(place, d, tiles, depth)
        there = pl.ds(pl.multiple_of(half * rows + row, depth), depth)
        keep = keep_ref[tile, there, :]
        for field in range(fields):
            sums_ref[field, tile, pl.ds(row, depth), :] = chunk[field] * keep
    grad_ref[...] = jnp.dot(
        sums_ref[...].reshape(fields * tiles * rows, width),
        matrix_ref[...],
        preferred_element_type=F32,
    ).reshape(grad_ref.shape)
    response = response_ref[pl.ds(pl.multiple_of((2 * band + half) * rows, rows), rows), :]
    line = lax.broadcasted_iota(jnp.int32, (rows, width), 0)
    sources = []
    for tile in range(tiles):
        ra = dec = src = first = last = 0.0
        for field in range(fields):
            share = share_ref[field]
            wide = sums_ref[field, tile].astype(F32)
            weight = wiener_ref[field, tile, here, :].astype(F32) * share
            above, below = pltpu.roll(wide, rows - 1, 0), pltpu.roll(wide, 1, 0)
            above_fill = below_fill = 0.0
            if late:
                near = early_sums_ref[field, tile].astype(F32)
                above_fill = jnp.where(half == 0, near[:1], 0.0)
                below_fill = jnp.where(half == 1, near[rows - 1 :], 0.0)
                beside = wiener_ref[field, tile, other, :].astype(F32) * share
                last = last + 0.5 * beside[rows - 1 :] * wide[:1]
                first = first - 0.5 * beside[:1] * wide[rows - 1 :]
            above = jnp.where(line == rows - 1, above_fill, above)
            below = jnp.where(line == 0, below_fill, below)
            ra = ra + weight * grad_ref[field, tile]
            dec = dec + weight * ((above - below) * 0.5)
            src = src + weight * wide
        high = ra.astype(BF16)
        ra_ref[tile, 0] = high
        ra_ref[tile, 1] = (ra - high.astype(F32)).astype(BF16)
        sources.append(response * src)
        if late:
            early_dec = early_dec_ref[tile]
            early_dec = early_dec + jnp.where((line == rows - 1) & (half == 1), last, 0.0)
            early_dec = early_dec + jnp.where((line == 0) & (half == 0), first, 0.0)
            dec_ref[tile, here, :] = dec
            dec_ref[tile, other, :] = early_dec
        else:
            early_dec_ref[tile] = dec
    both = jnp.dot(
        ra_ref[...].reshape(tiles * 2 * rows, width), matrix_ref[...], preferred_element_type=F32
    ).reshape(tiles, 2, rows, width)
    for tile in range(tiles):
        part = -(both[tile, 0] + both[tile, 1]) - sources[tile]
        if late:
            columns = pl.ds(tile * width, width)
            out_ref[here, columns] = part
            out_ref[other, columns] = early_part_ref[tile]
            out_ref[:, columns] = out_ref[:, columns] - slope(dec_ref[tile])
        else:
            part_ref[tile] = part


def half_call(splits, order, shares, keep, wiener, matrix, response, chunks, early):
    fields, depth, width = chunks[0].shape
    tiles, all_rows, _ = keep.shape
    rows = all_rows // 2
    late = early is not None
    sums = (fields, tiles, rows, width)
    scratch = [pltpu.VMEM(sums, F32), pltpu.VMEM((tiles, 2, rows, width), BF16)]
    if late:
        out_shape = jax.ShapeDtypeStruct((all_rows, tiles * width), F32)
        scratch = [pltpu.VMEM(sums, BF16), pltpu.VMEM((tiles, all_rows, width), F32)] + scratch
    else:
        part = jax.ShapeDtypeStruct((tiles, rows, width), F32)
        out_shape = [jax.ShapeDtypeStruct(sums, BF16), part, part]
    operands = [keep, wiener, matrix, response, *chunks, *(early or [])]
    return pl.pallas_call(
        functools.partial(half_kernel, splits, order, late),
        out_shape=out_shape,
        in_specs=[SMEM] + [VMEM] * len(operands),
        out_specs=VMEM if late else [VMEM] * 3,
        scratch_shapes=scratch,
        compiler_params=PARAMS,
        cost_estimate=cost(2 * (fields + 2) * tiles * rows * width * width, 16 * tiles * rows * width),
        name="late_half" if late else "early_half",
    )(shares, *operands)


def slope(values):
    rows = values.shape[0]
    line = lax.broadcasted_iota(jnp.int32, values.shape, 0)
    above = jnp.where(line == rows - 1, 0.0, pltpu.roll(values, rows - 1, 0))
    below = jnp.where(line == 0, 0.0, pltpu.roll(values, 1, 0))
    return (above - below) * 0.5


def edges_kernel(splits, order, keep_ref, wiener_ref, *refs):
    chunks = refs[:splits]
    bands = lax.axis_size("sim") // splits
    outs = refs[-1:] if bands == 2 else refs[-2:]
    fields, tiles, _, width = outs[0].shape
    depth = chunks[0].shape[1]
    rows = keep_ref.shape[1]
    place, band = place_and_band(splits)
    for side, out_ref in enumerate(outs):
        upper = (band == 0) if bands == 2 else (side == 1)
        for d, chunk in zip(order, chunks):
            half, row, tile = slot_at(place, d, tiles, depth)
            edge_row = jnp.where(upper, rows - depth, 0)

            @pl.when(half * (rows // 2) + row == edge_row)
            def _():
                keep = keep_ref[tile, pl.ds(pl.multiple_of(edge_row, depth), depth), :]
                for field in range(fields):
                    pixels = (chunk[field] * keep).astype(F32)
                    outer = jnp.where(upper, pixels[depth - 1 :], pixels[:1])
                    inner = jnp.where(upper, pixels[depth - 2 : depth - 1], pixels[1:2])
                    weight = wiener_ref[field, tile].astype(F32)
                    weight = jnp.where(upper, weight[rows - 1 :], weight[:1])
                    out_ref[field, tile] = jnp.concatenate([outer, inner, weight], axis=0).astype(BF16)


def edges(splits, order, keep, wiener, chunks, after):
    fields, depth, width = chunks[0].shape
    count = 1 if lax.axis_size("sim") // splits == 2 else 2
    shape = jax.ShapeDtypeStruct((fields, keep.shape[0], 3, width), BF16)
    return pl.pallas_call(
        functools.partial(edges_kernel, splits, order),
        out_shape=[shape] * count,
        in_specs=[VMEM] * (splits + 2) + [ANY] * len(after),
        out_specs=[VMEM] * count,
        compiler_params=PARAMS,
        cost_estimate=cost(0, 2 * splits * fields * depth * width),
        name="edges",
    )(keep, wiener, *chunks, *after)


def rim_kernel(sides_ref, flags_ref, share_ref, out_in_ref, *refs):
    out_ref = refs[-1]
    block, columns = out_ref.shape
    out_ref[...] = out_in_ref[...]
    step = pl.program_id(0)
    side = sides_ref[step]
    line = lax.broadcasted_iota(jnp.int32, (block, 1), 0)
    outermost = line == side * (block - 1)
    next_row = line == 1 + side * (block - 3)
    for number in range(len(refs) // 2):
        own_ref, far_ref = refs[2 * number], refs[2 * number + 1]
        fields, tiles, _, width = own_ref.shape

        @pl.when((step == number) & (flags_ref[number] > 0))
        def _():
            for tile in range(tiles):
                inner = outer = 0.0
                for field in range(fields):
                    share = share_ref[field] * 0.25
                    own = own_ref[field, tile].astype(F32)
                    far = far_ref[field, tile].astype(F32)
                    inner += own[2:3] * far[0:1] * share
                    outer += far[2:3] * (own[0:1] - far[1:2]) * share
                part = pl.ds(tile * width, width)
                change = jnp.where(outermost, outer, 0.0) - jnp.where(next_row, inner, 0.0)
                out_ref[:, part] = out_ref[:, part] + change


def rim(sides, flags, shares, out, rims):
    rows, columns = out.shape
    block = pl.BlockSpec((8, columns), lambda step, sides, *_: (sides[step] * (rows // 8 - 1), 0))

    def whole(array):
        zeros = (0,) * array.ndim
        return pl.BlockSpec(array.shape, lambda *_: zeros)

    return pl.pallas_call(
        rim_kernel,
        out_shape=jax.ShapeDtypeStruct(out.shape, out.dtype),
        grid_spec=pltpu.PrefetchScalarGridSpec(
            num_scalar_prefetch=3,
            grid=(sides.shape[0],),
            in_specs=[block] + [whole(array) for array in rims],
            out_specs=block,
        ),
        input_output_aliases={3: 0},
        compiler_params=PARAMS,
        cost_estimate=cost(0, 64 * columns),
        name="rim",
    )(sides, flags, shares, out, *rims)


def distinct_kernel(index_ref, count_ref, distinct_ref, share_ref):
    uses = index_ref.shape[0]
    share_ref[0] = jnp.float32(1.0)
    for number in range(uses):
        distinct_ref[number] = index_ref[0]
        share_ref[number + 1] = jnp.float32(0.0)
    count = jnp.int32(0)
    for number in range(uses):
        same = [(index_ref[other] == index_ref[number]).astype(jnp.int32) for other in range(uses)]
        new = sum(same[:number], jnp.int32(0)) == 0
        times = sum(same, jnp.int32(0)).astype(F32)

        @pl.when(new)
        def _():
            distinct_ref[count] = index_ref[number]
            share_ref[count + 1] = times * (-1.0 / uses)

        count = count + new.astype(jnp.int32)
    count_ref[0] = count


def distinct_fields(sim_index):
    uses = sim_index.shape[0]
    return pl.pallas_call(
        distinct_kernel,
        out_shape=[
            jax.ShapeDtypeStruct((1,), jnp.int32),
            jax.ShapeDtypeStruct((uses,), jnp.int32),
            jax.ShapeDtypeStruct((uses + 1,), F32),
        ],
        in_specs=[SMEM],
        out_specs=[SMEM] * 3,
        name="distinct",
    )(sim_index)


def estimate(
    sky_maps,
    ivf_maps,
    sim_sky,
    sim_ivf,
    ra_wiener,
    ra_gradient,
    pair_table,
    sim_index,
    shares,
    source_pixels,
    response,
):
    splits = pair_table.shape[0]
    axis_count = lax.axis_size("sim")
    bands = axis_count // splits
    place, band = place_and_band(splits)
    rows, columns = sky_maps.shape
    width = ra_gradient.shape[0]
    depth = rows * (columns // width) // splits

    def swap(block, d):
        pairs = [
            (g * bands + u, (g ^ d) * bands + u) for g in range(splits) for u in range(bands)
        ]
        return lax.ppermute(block, "sim", pairs)

    def exchange(blocks):
        moved = {d: swap(blocks[d], d) for d in EARLY + LATE}
        return {0: blocks[0], **moved}

    def neighbours(edge):
        if bands == 2:
            pairs = [((k + 1) % axis_count, k) if k % 2 else ((k - 1) % axis_count, k)
                     for k in range(axis_count)]
            return [edge[0], lax.ppermute(edge[0], "sim", pairs)]
        ahead = [(k, (k + 1) % axis_count) for k in range(axis_count)]
        back = [((k + 1) % axis_count, k) for k in range(axis_count)]
        below, above = lax.ppermute(edge[1], "sim", ahead), lax.ppermute(edge[0], "sim", back)
        return [edge[0], below, edge[1], above]

    if bands == 2:
        sides, flags = (1 - band)[None], jnp.ones((1,), jnp.int32)
    else:
        sides = jnp.arange(2, dtype=jnp.int32)
        flags = jnp.stack([band > 0, band < bands - 1]).astype(jnp.int32)

    slots = place ^ jnp.arange(splits, dtype=jnp.int32)
    split_of = (slots - (lax.axis_index("sim") % bands < bands // 2)) % splits
    pairs = jnp.where(split_of[:, None] == split_of[None], 0, pair_table[split_of][:, split_of])
    weights = jnp.kron(pairs.astype(F32), jnp.eye(depth, dtype=F32)).astype(BF16)

    arrived = exchange(pack(splits, sim_index, ivf_maps, sim_ivf, depth, width))
    wiener = wiener_fields(sim_index, sky_maps, sim_sky, ra_wiener, [])
    keep = keep_mask(source_pixels, band, rows, columns, width, [])
    sums = exchange(mix(weights, arrived, []))
    shared = keep, wiener, ra_gradient, response[:, None]
    early, late = (0,) + EARLY, LATE
    early_results = half_call(splits, early, shares, *shared, [sums[d] for d in early], None)
    order = early + late
    edge = edges(splits, order, keep, wiener, [sums[d] for d in order], early_results[1:2])
    rims = neighbours(edge)
    out = half_call(splits, late, shares, *shared, [sums[d] for d in late], early_results)
    return rim(sides, flags, shares, out, rims)


def on_device(
    sky_maps,
    ivf_maps,
    sim_sky,
    sim_ivf,
    ra_wiener,
    ra_gradient,
    pair_table,
    sim_index,
    source_pixels,
    response,
):
    uses = sim_index.shape[0]
    count, distinct, shares = distinct_fields(sim_index)
    sizes = range(max(1, uses - 2), uses + 1)

    def of_size(size):
        def run(distinct, shares):
            return estimate(
                sky_maps,
                ivf_maps,
                sim_sky,
                sim_ivf,
                ra_wiener,
                ra_gradient,
                pair_table,
                distinct[:size],
                shares[: size + 1],
                source_pixels,
                response,
            )

        return run

    branch = jnp.clip(count[0] - sizes[0], 0, len(sizes) - 1)
    return lax.switch(branch, [of_size(size) for size in sizes], distinct, shares)


def solution(mesh):
    in_specs = (
        P(("patch", "sim"), None),
        P(("patch", "sim"), None),
        P(None, ("patch", "sim"), None),
        P(None, ("patch", "sim"), None),
        P(),
        P(),
        P(),
        P(),
        P("patch"),
        P("patch"),
    )
    out_specs = P(("patch", "sim"), None)
    return jax.shard_map(
        on_device, mesh=mesh, in_specs=in_specs, out_specs=out_specs, check_vma=False
    )
```

```python
import functools

import jax
import jax.numpy as jnp
from jax import lax
from jax.experimental import pallas as pl
from jax.experimental.pallas import tpu as pltpu
from jax.sharding import PartitionSpec as P

PIXEL_CHUNK = 1024
LOW_COLUMNS = 256
MIB = 1024 * 1024

F32 = jnp.float32
BF16 = jnp.bfloat16
SMEM = pl.BlockSpec(memory_space=pltpu.SMEM)
VMEM = pl.BlockSpec(memory_space=pltpu.VMEM)
ANY = pl.BlockSpec(memory_space=pl.ANY)
WIDE_PARAMS = pltpu.CompilerParams(vmem_limit_bytes=60 * MIB)
PARAMS = pltpu.CompilerParams(vmem_limit_bytes=24 * MIB)

EARLY = (7, 1, 6)
LATE = (2, 3, 5, 4)


def cost(flops, bytes_accessed):
    return pl.CostEstimate(flops=int(flops), bytes_accessed=int(bytes_accessed), transcendentals=0)


def place_and_band(splits):
    count = lax.axis_size("sim")
    bands = count // splits
    device = lax.axis_index("sim")
    logical = lax.rem(device + (count - bands // 2), count)
    return lax.div(device, bands), lax.rem(logical, bands)


def slot_at(place, d, tiles, depth):
    slot = lax.bitwise_xor(place, d)
    block = lax.div(slot, tiles)
    half = lax.bitwise_and(lax.bitwise_xor(block, lax.div(block, 2)), 1)
    return half, pl.multiple_of(lax.div(block, 2) * depth, depth), lax.rem(slot, tiles)


def keep_kernel(rows, width, a_ref, b_ref, *refs):
    keep_ref, total = refs[-2:]
    pixels = a_ref.shape[1]
    tall = total.shape[0]
    total[...] = jnp.zeros_like(total)

    @pl.loop(0, pixels // PIXEL_CHUNK)
    def _(step):
        part = pl.ds(pl.multiple_of(step * PIXEL_CHUNK, PIXEL_CHUNK), PIXEL_CHUNK)
        high = lax.broadcasted_iota(jnp.int32, (tall, PIXEL_CHUNK), 0) == a_ref[:, part]
        low = lax.broadcasted_iota(jnp.int32, (LOW_COLUMNS, PIXEL_CHUNK), 0) == b_ref[:, part]
        total[...] += lax.dot_general(
            high.astype(F32).astype(BF16),
            low.astype(F32).astype(BF16),
            (((1,), (1,)), ((), ())),
            preferred_element_type=F32,
        )

    per_tile = width // LOW_COLUMNS
    for block in range(tall // rows):
        tile, piece = block // per_tile, block % per_tile
        count = total[block * rows : (block + 1) * rows, :]
        keep_ref[tile, :, piece * LOW_COLUMNS : (piece + 1) * LOW_COLUMNS] = jnp.where(
            count > 0, 0.0, 1.0
        ).astype(BF16)


def keep_mask(source_pixels, band_index, rows, columns, width, after):
    offsets = source_pixels - band_index * rows * columns
    inside = (offsets >= 0) & (offsets < rows * columns)
    row, column = offsets // columns, offsets % columns
    a = jnp.where(inside, (column // LOW_COLUMNS) * rows + row, -1)
    b = column % LOW_COLUMNS
    pixels = source_pixels.shape[0]
    extra = -pixels % PIXEL_CHUNK
    a = jnp.pad(a, (0, extra), constant_values=-1)[None]
    b = jnp.pad(b, (0, extra))[None]
    tall = columns // LOW_COLUMNS * rows
    return pl.pallas_call(
        functools.partial(keep_kernel, rows, width),
        out_shape=jax.ShapeDtypeStruct((columns // width, rows, width), BF16),
        in_specs=[VMEM, VMEM] + [ANY] * len(after),
        out_specs=VMEM,
        scratch_shapes=[pltpu.VMEM((tall, LOW_COLUMNS), F32)],
        compiler_params=PARAMS,
        cost_estimate=cost(2 * tall * LOW_COLUMNS * (pixels + extra), 4 * rows * columns),
        name="keep",
    )(a, b, *after)


def rim_sides(splits, band):
    if lax.axis_size("sim") // splits == 2:
        return [band == 0]
    return [False, True]


def as_rows(values, rows, width):
    values = values + [jnp.zeros((rows - len(values), width), F32)]
    return jnp.concatenate(values, axis=0).astype(BF16)


def wiener_kernel(splits, index_ref, share_ref, sky_ref, sim_ref, matrix_ref, out_ref, *refs):
    scale_ref, edge_refs, (held, sems) = refs[0], refs[1:-2], refs[-2:]
    fields, tiles, rows, width = out_ref.shape
    copies = [pltpu.make_async_copy(sky_ref, held.at[0], sems.at[0])]
    for field in range(1, fields):
        source = sim_ref.at[index_ref[field - 1]]
        copies.append(pltpu.make_async_copy(source, held.at[field], sems.at[field]))
    for copy in copies:
        copy.start()
    for copy in copies:
        copy.wait()
    for tile in range(tiles):
        values = held[:, :, tile * width : (tile + 1) * width].reshape(fields * rows, width)
        result = jnp.dot(values, matrix_ref[...], preferred_element_type=F32).astype(BF16)
        out_ref[:, tile] = result.reshape(fields, rows, width)
    for field in range(fields):
        scale_ref[field : field + 1, :] = jnp.full((1, scale_ref.shape[1]), share_ref[field], F32)
    _, band = place_and_band(splits)
    for upper, edge_ref in zip(rim_sides(splits, band), edge_refs):
        for tile in range(tiles):
            picked = []
            for field in range(fields):
                low = out_ref[field, tile, :8, :].astype(F32)[:1]
                high = out_ref[field, tile, rows - 8 :, :].astype(F32)[7:]
                picked.append(jnp.where(upper, high, low) * share_ref[field])
            columns = pl.ds(tile * width, width)
            edge_ref[:, columns] = as_rows(picked, edge_ref.shape[0], width)


def rim_shapes(splits, fields, columns):
    count = 1 if lax.axis_size("sim") // splits == 2 else 2
    return [jax.ShapeDtypeStruct((-(-(fields + 1) // 8) * 8, columns), BF16)] * count


def wiener_fields(splits, sim_index, shares, sky_maps, sim_sky, matrix):
    rows, columns = sky_maps.shape
    width = matrix.shape[0]
    fields = sim_index.shape[0] + 1
    rims = rim_shapes(splits, fields, columns)
    wiener, scale, *edge = pl.pallas_call(
        functools.partial(wiener_kernel, splits),
        out_shape=[
            jax.ShapeDtypeStruct((fields, columns // width, rows, width), BF16),
            jax.ShapeDtypeStruct((-(-fields // 8) * 8, 128), F32),
            *rims,
        ],
        in_specs=[SMEM, SMEM, ANY, ANY, VMEM],
        out_specs=[VMEM] * (2 + len(rims)),
        scratch_shapes=[
            pltpu.VMEM((fields, rows, columns), BF16),
            pltpu.SemaphoreType.DMA((fields,)),
        ],
        compiler_params=PARAMS,
        cost_estimate=cost(2 * fields * rows * columns * width, 4 * fields * rows * columns),
        name="wiener",
    )(sim_index, shares, sky_maps, sim_sky, matrix)
    return wiener, scale, edge


def pack_kernel(splits, order, index_ref, ivf_ref, sim_ref, *refs):
    outs, held, sems = refs[: len(order)], refs[-2], refs[-1]
    fields, depth, width = outs[0].shape
    rows, columns = ivf_ref.shape
    place, _ = place_and_band(splits)

    def region(d):
        half, row, tile = slot_at(place, d, columns // width, depth)
        part = pl.ds(pl.multiple_of(half * (rows // 2) + row, depth), depth)
        return part, pl.ds(pl.multiple_of(tile * width, width), width)

    alone = len(order) == 1
    wanted = region(order[0]) if alone else (slice(None), slice(None))
    copies = [pltpu.make_async_copy(ivf_ref.at[wanted], held.at[0], sems.at[0])]
    for field in range(1, fields):
        source = sim_ref.at[(index_ref[field - 1],) + wanted]
        copies.append(pltpu.make_async_copy(source, held.at[field], sems.at[field]))
    for copy in copies:
        copy.start()
    for field in range(fields):
        copies[field].wait()
        for d, out in zip(order, outs):
            out[field] = held[field] if alone else held[(field,) + region(d)]


def pack(splits, order, sim_index, ivf_maps, sim_ivf, depth, width):
    fields = sim_index.shape[0] + 1
    held = (depth, width) if len(order) == 1 else ivf_maps.shape
    chunks = pl.pallas_call(
        functools.partial(pack_kernel, splits, order),
        out_shape=[jax.ShapeDtypeStruct((fields, depth, width), BF16)] * len(order),
        in_specs=[SMEM, ANY, ANY],
        out_specs=[VMEM] * len(order),
        scratch_shapes=[
            pltpu.VMEM((fields,) + held, BF16),
            pltpu.SemaphoreType.DMA((fields,)),
        ],
        compiler_params=WIDE_PARAMS,
        cost_estimate=cost(0, 4 * len(order) * fields * depth * width),
        name="pack",
    )(sim_index, ivf_maps, sim_ivf)
    return dict(zip(order, chunks))


def prepare_kernel(splits, pair_ref, own_ref, weights_ref, held_ref, sem):
    copy = pltpu.make_async_copy(own_ref, held_ref, sem)
    copy.start()
    size = weights_ref.shape[0]
    depth = size // splits
    place, band = place_and_band(splits)
    bands = lax.axis_size("sim") // splits
    shift = (band >= bands - bands // 2).astype(jnp.int32)
    split_of = [lax.rem(lax.bitwise_xor(place, d) + splits - shift, splits) for d in range(splits)]
    row = lax.broadcasted_iota(jnp.int32, (size, size), 0)
    column = lax.broadcasted_iota(jnp.int32, (size, size), 1)
    total = jnp.zeros((size, size), F32)
    for d in range(splits):
        for e in range(splits):
            if d != e:
                here = (lax.div(row, depth) == d) & (lax.div(column, depth) == e)
                value = pair_ref[split_of[d], split_of[e]].astype(F32)
                total = jnp.where(here, value, total)
    same = lax.rem(row, depth) == lax.rem(column, depth)
    weights_ref[...] = jnp.where(same, total, 0.0).astype(BF16)
    copy.wait()


def prepare(pair_table, own):
    splits = pair_table.shape[0]
    size = splits * own.shape[1]
    return pl.pallas_call(
        functools.partial(prepare_kernel, splits),
        out_shape=[
            jax.ShapeDtypeStruct((size, size), BF16),
            jax.ShapeDtypeStruct(own.shape, BF16),
        ],
        in_specs=[SMEM, ANY],
        out_specs=[VMEM, VMEM],
        scratch_shapes=[pltpu.SemaphoreType.DMA],
        compiler_params=PARAMS,
        cost_estimate=cost(splits * splits * size * size, 4 * own.size),
        name="prepare",
    )(pair_table, own)


def mix_kernel(order, weights_ref, *refs):
    parts = len(order)
    chunks, outs = refs[:parts], refs[parts:]
    fields, depth, _ = chunks[0].shape
    for field in range(fields):
        stacked = jnp.concatenate([chunks[order.index(d)][field] for d in range(parts)], axis=0)
        mixed = jnp.dot(weights_ref[...], stacked, preferred_element_type=F32).astype(BF16)
        for d in range(parts):
            outs[d][field] = mixed[d * depth : (d + 1) * depth]


def mix(weights, chunks):
    order = EARLY + LATE + (0,)
    parts = len(chunks)
    shape = chunks[0].shape
    size = shape[0] * shape[1] * shape[2]
    return pl.pallas_call(
        functools.partial(mix_kernel, order),
        out_shape=[jax.ShapeDtypeStruct(shape, BF16)] * parts,
        in_specs=[VMEM] * (parts + 1),
        out_specs=[VMEM] * parts,
        compiler_params=PARAMS,
        cost_estimate=cost(2 * parts * size * weights.shape[0], 4 * parts * size),
        name="mix",
    )(weights, *[chunks[d] for d in order])


def half_kernel(
    splits, order, late, keep_ref, wiener_ref, scale_ref, matrix_ref, response_ref, *refs
):
    chunks = refs[: len(order)]
    fields, depth, width = chunks[0].shape
    if late:
        early_sums_ref, early_dec_ref = refs[len(order) : len(order) + 2]
        part_ref, dec_ref, sums_ref, grad_ref, ra_ref = refs[len(order) + 2 :]
    else:
        sums_ref, part_ref, early_dec_ref, grad_ref, ra_ref = refs[len(order) :]
    tiles, rows = sums_ref.shape[1:3]
    place, band = place_and_band(splits)
    half = slot_at(place, order[0], tiles, depth)[0]
    here = pl.ds(pl.multiple_of(half * rows, rows), rows)
    other = pl.ds(pl.multiple_of((1 - half) * rows, rows), rows)
    for d, chunk in zip(order, chunks):
        _, row, tile = slot_at(place, d, tiles, depth)
        there = pl.ds(pl.multiple_of(half * rows + row, depth), depth)
        keep = keep_ref[tile, there, :]
        for field in range(fields):
            sums_ref[field, tile, pl.ds(row, depth), :] = chunk[field] * keep
    grad_ref[...] = jnp.dot(
        sums_ref[...].reshape(fields * tiles * rows, width),
        matrix_ref[...],
        preferred_element_type=F32,
    ).reshape(grad_ref.shape)
    response = response_ref[pl.ds(pl.multiple_of((2 * band + half) * rows, rows), rows), :]
    line = lax.broadcasted_iota(jnp.int32, (rows, width), 0)
    sources = []
    for tile in range(tiles):
        ra = dec = src = first = last = 0.0
        for field in range(fields):
            wide = sums_ref[field, tile].astype(F32)
            share = scale_ref[field : field + 1, :1]
            weight = wiener_ref[field, tile, here, :].astype(F32) * share
            above, below = pltpu.roll(wide, rows - 1, 0), pltpu.roll(wide, 1, 0)
            above_fill = below_fill = 0.0
            if late:
                near = early_sums_ref[field, tile].astype(F32)
                above_fill = jnp.where(half == 0, near[:1], 0.0)
                below_fill = jnp.where(half == 1, near[rows - 1 :], 0.0)
                beside = wiener_ref[field, tile, other, :].astype(F32) * share
                last = last + 0.5 * beside[rows - 1 :] * wide[:1]
                first = first - 0.5 * beside[:1] * wide[rows - 1 :]
            above = jnp.where(line == rows - 1, above_fill, above)
            below = jnp.where(line == 0, below_fill, below)
            ra = ra + weight * grad_ref[field, tile]
            dec = dec + weight * ((above - below) * 0.5)
            src = src + weight * wide
        high = ra.astype(BF16)
        ra_ref[tile, 0] = high
        ra_ref[tile, 1] = (ra - high.astype(F32)).astype(BF16)
        sources.append(response * src)
        if late:
            early_dec = early_dec_ref[tile]
            early_dec = early_dec + jnp.where((line == rows - 1) & (half == 1), last, 0.0)
            early_dec = early_dec + jnp.where((line == 0) & (half == 0), first, 0.0)
            dec_ref[tile, here, :] = dec
            dec_ref[tile, other, :] = early_dec
        else:
            early_dec_ref[tile] = dec
    both = jnp.dot(
        ra_ref[...].reshape(tiles * 2 * rows, width), matrix_ref[...], preferred_element_type=F32
    ).reshape(tiles, 2, rows, width)
    for tile in range(tiles):
        part_ref[tile] = -(both[tile, 0] + both[tile, 1]) - sources[tile]


def half_call(splits, order, keep, wiener, scale, matrix, response, chunks, early):
    fields, depth, width = chunks[0].shape
    tiles, all_rows, _ = keep.shape
    rows = all_rows // 2
    late = early is not None
    sums = (fields, tiles, rows, width)
    scratch = [pltpu.VMEM(sums, F32), pltpu.VMEM((tiles, 2, rows, width), BF16)]
    part = jax.ShapeDtypeStruct((tiles, rows, width), F32)
    if late:
        out_shape = [part, jax.ShapeDtypeStruct((tiles, all_rows, width), F32)]
        scratch = [pltpu.VMEM(sums, BF16)] + scratch
    else:
        out_shape = [jax.ShapeDtypeStruct(sums, BF16), part, part]
    operands = [keep, wiener, scale, matrix, response, *chunks, *(early or [])]
    return pl.pallas_call(
        functools.partial(half_kernel, splits, order, late),
        out_shape=out_shape,
        in_specs=[VMEM] * len(operands),
        out_specs=[VMEM] * len(out_shape),
        scratch_shapes=scratch,
        compiler_params=PARAMS,
        cost_estimate=cost(2 * (fields + 2) * tiles * rows * width * width, 16 * tiles * rows * width),
        name="late_half" if late else "early_half",
    )(*operands)


def slope(values):
    rows = values.shape[0]
    line = lax.broadcasted_iota(jnp.int32, values.shape, 0)
    above = jnp.where(line == rows - 1, 0.0, pltpu.roll(values, rows - 1, 0))
    below = jnp.where(line == 0, 0.0, pltpu.roll(values, 1, 0))
    return (above - below) * 0.5


def edges_kernel(splits, order, keep_ref, *refs):
    place, band = place_and_band(splits)
    sides = rim_sides(splits, band)
    weights, chunks = refs[: len(sides)], refs[len(sides) : len(sides) + splits]
    outs, (block, outermost, inner) = refs[-3 - len(sides) : -3], refs[-3:]
    fields, depth, width = chunks[0].shape
    tiles, rows, _ = keep_ref.shape
    outermost[...] = jnp.zeros_like(outermost)
    inner[...] = jnp.zeros_like(inner)
    for upper, weight_ref, out_ref in zip(sides, weights, outs):
        edge_row = jnp.where(upper, rows - depth, 0)
        there = pl.ds(pl.multiple_of(edge_row, depth), depth)
        for d, chunk in zip(order, chunks):
            half, row, tile = slot_at(place, d, tiles, depth)

            @pl.when(half * (rows // 2) + row == edge_row)
            def _():
                keep = keep_ref[tile, there, :]
                for field in range(fields):
                    block[...] = (chunk[field] * keep).astype(F32)
                    last = jnp.where(upper, depth - 1, 0)
                    outermost[field : field + 1, :] = block[pl.ds(last, 1), :]
                    inner[field : field + 1, :] = block[pl.ds(jnp.where(upper, depth - 2, 1), 1), :]
                columns = pl.ds(pl.multiple_of(tile * width, width), width)
                beyond = weight_ref[:, columns].astype(F32) * inner[...]
                outermost[fields : fields + 1, :] = jnp.sum(beyond, axis=0, keepdims=True)
                out_ref[:, columns] = outermost[...].astype(BF16)


def edges(splits, order, keep, w_edge, chunks, after):
    fields, depth, width = chunks[0].shape
    rims = rim_shapes(splits, fields, keep.shape[0] * width)
    rows = rims[0].shape[0]
    return pl.pallas_call(
        functools.partial(edges_kernel, splits, order),
        out_shape=rims,
        in_specs=[VMEM] * (splits + 1 + len(rims)) + [ANY] * len(after),
        out_specs=[VMEM] * len(rims),
        scratch_shapes=[
            pltpu.VMEM((depth, width), F32),
            pltpu.VMEM((rows, width), F32),
            pltpu.VMEM((rows, width), F32),
        ],
        compiler_params=PARAMS,
        cost_estimate=cost(0, 2 * splits * fields * depth * width),
        name="edges",
    )(keep, *w_edge, *chunks, *after)


def finish_kernel(splits, fields, early_ref, late_ref, dec_ref, *refs):
    rims, (out_ref, sums) = refs[:-2], refs[-2:]
    tiles, rows, width = dec_ref.shape
    half_rows = rows // 2
    place, band = place_and_band(splits)
    bands = lax.axis_size("sim") // splits
    half = slot_at(place, 0, tiles, rows * tiles // splits)[0]
    here = pl.ds(pl.multiple_of(half * half_rows, half_rows), half_rows)
    other = pl.ds(pl.multiple_of((1 - half) * half_rows, half_rows), half_rows)
    line = lax.broadcasted_iota(jnp.int32, (8, 1), 0)
    sides = [(band > 0, band == 0)] if bands == 2 else [(band > 0, False), (False, band < bands - 1)]
    for tile in range(tiles):
        sums[tile, here, :] = early_ref[tile]
        sums[tile, other, :] = late_ref[tile]
        sums[tile] = sums[tile] - slope(dec_ref[tile])
        columns = pl.ds(tile * width, width)
        for number, (low, high) in enumerate(sides):
            own_w, far_w, own, far = [
                ref[:, columns].astype(F32) for ref in rims[4 * number : 4 * number + 4]
            ]
            inner = 0.25 * jnp.sum(own_w * far, axis=0, keepdims=True)
            outer = jnp.sum(far_w * own, axis=0, keepdims=True) - far[fields : fields + 1]
            outer = 0.25 * outer
            first, last = sums[tile, :8, :], sums[tile, rows - 8 :, :]
            first += jnp.where((line == 0) & low, outer, 0.0)
            first -= jnp.where((line == 1) & low, inner, 0.0)
            last += jnp.where((line == 7) & high, outer, 0.0)
            last -= jnp.where((line == 6) & high, inner, 0.0)
            sums[tile, :8, :] = first
            sums[tile, rows - 8 :, :] = last
        out_ref[:, columns] = sums[tile]


def finish(splits, fields, early_part, late_part, dec, rims):
    tiles, rows, width = dec.shape
    return pl.pallas_call(
        functools.partial(finish_kernel, splits, fields),
        out_shape=pltpu.HBM((rows, tiles * width), F32),
        in_specs=[VMEM] * (3 + len(rims)),
        out_specs=VMEM,
        scratch_shapes=[pltpu.VMEM((tiles, rows, width), F32)],
        compiler_params=PARAMS,
        cost_estimate=cost(0, 12 * tiles * rows * width),
        name="finish",
    )(early_part, late_part, dec, *rims)


def distinct_kernel(index_ref, count_ref, distinct_ref, share_ref):
    uses = index_ref.shape[0]
    share_ref[0] = jnp.float32(1.0)
    for number in range(uses):
        distinct_ref[number] = index_ref[0]
        share_ref[number + 1] = jnp.float32(0.0)
    count = jnp.int32(0)
    for number in range(uses):
        same = [(index_ref[other] == index_ref[number]).astype(jnp.int32) for other in range(uses)]
        new = sum(same[:number], jnp.int32(0)) == 0
        times = sum(same, jnp.int32(0)).astype(F32)

        @pl.when(new)
        def _():
            distinct_ref[count] = index_ref[number]
            share_ref[count + 1] = times * (-1.0 / uses)

        count = count + new.astype(jnp.int32)
    count_ref[0] = count


def distinct_fields(sim_index):
    uses = sim_index.shape[0]
    return pl.pallas_call(
        distinct_kernel,
        out_shape=[
            jax.ShapeDtypeStruct((1,), jnp.int32),
            jax.ShapeDtypeStruct((uses,), jnp.int32),
            jax.ShapeDtypeStruct((uses + 1,), F32),
        ],
        in_specs=[SMEM],
        out_specs=[SMEM] * 3,
        name="distinct",
    )(sim_index)


def estimate(
    sky_maps,
    ivf_maps,
    sim_sky,
    sim_ivf,
    ra_wiener,
    ra_gradient,
    pair_table,
    sim_index,
    shares,
    source_pixels,
    response,
):
    splits = pair_table.shape[0]
    axis_count = lax.axis_size("sim")
    bands = axis_count // splits
    place, band = place_and_band(splits)
    rows, columns = sky_maps.shape
    width = ra_gradient.shape[0]
    depth = rows * (columns // width) // splits

    def swap(block, d):
        pairs = [
            (g * bands + u, (g ^ d) * bands + u) for g in range(splits) for u in range(bands)
        ]
        return lax.ppermute(block, "sim", pairs)

    def exchange(blocks):
        moved = {d: swap(blocks[d], d) for d in EARLY + LATE}
        return {0: blocks[0], **moved}

    def neighbours(edge):
        if bands == 2:
            pairs = [((k + 1) % axis_count, k) if k % 2 else ((k - 1) % axis_count, k)
                     for k in range(axis_count)]
            return [edge[0], lax.ppermute(edge[0], "sim", pairs)]
        ahead = [(k, (k + 1) % axis_count) for k in range(axis_count)]
        back = [((k + 1) % axis_count, k) for k in range(axis_count)]
        below, above = lax.ppermute(edge[1], "sim", ahead), lax.ppermute(edge[0], "sim", back)
        return [edge[0], below, edge[1], above]

    first, rest = EARLY[:1], (0,) + EARLY[1:] + LATE
    sent = pack(splits, first, sim_index, ivf_maps, sim_ivf, depth, width)
    sent.update(pack(splits, rest, sim_index, ivf_maps, sim_ivf, depth, width))
    arrived = exchange(sent)
    wiener, scale, w_edge = wiener_fields(splits, sim_index, shares, sky_maps, sim_sky, ra_wiener)
    w_rims = neighbours(w_edge)
    keep = keep_mask(source_pixels, band, rows, columns, width, [])
    weights, arrived[0] = prepare(pair_table, arrived[0])
    sums = exchange(mix(weights, arrived))
    shared = keep, wiener, scale, ra_gradient, response[:, None]
    early, late = (0,) + EARLY, LATE
    early_results = half_call(splits, early, *shared, [sums[d] for d in early], None)
    order = early + late
    edge = edges(splits, order, keep, w_edge, [sums[d] for d in order], early_results[1:2])
    s_rims = neighbours(edge)
    rims = [rim for n in range(0, len(s_rims), 2) for rim in w_rims[n : n + 2] + s_rims[n : n + 2]]
    late_part, dec = half_call(
        splits, late, *shared, [sums[d] for d in late], early_results[::2]
    )
    return finish(splits, shares.shape[0], early_results[1], late_part, dec, rims)


def on_device(
    sky_maps,
    ivf_maps,
    sim_sky,
    sim_ivf,
    ra_wiener,
    ra_gradient,
    pair_table,
    sim_index,
    source_pixels,
    response,
):
    uses = sim_index.shape[0]
    count, distinct, shares = distinct_fields(sim_index)
    sizes = range(max(1, uses - 2), uses + 1)

    def of_size(size):
        def run(distinct, shares):
            return estimate(
                sky_maps,
                ivf_maps,
                sim_sky,
                sim_ivf,
                ra_wiener,
                ra_gradient,
                pair_table,
                distinct[:size],
                shares[: size + 1],
                source_pixels,
                response,
            )

        return run

    branch = jnp.clip(count[0] - sizes[0], 0, len(sizes) - 1)
    return lax.switch(branch, [of_size(size) for size in sizes], distinct, shares)


def solution(mesh):
    in_specs = (
        P(("patch", "sim"), None),
        P(("patch", "sim"), None),
        P(None, ("patch", "sim"), None),
        P(None, ("patch", "sim"), None),
        P(),
        P(),
        P(),
        P(),
        P("patch"),
        P("patch"),
    )
    out_specs = P(("patch", "sim"), None)
    return jax.shard_map(
        on_device, mesh=mesh, in_specs=in_specs, out_specs=out_specs, check_vma=False
    )
```

```python
import functools

import jax
import jax.numpy as jnp
from jax import lax
from jax.experimental import pallas as pl
from jax.experimental.pallas import tpu as pltpu
from jax.sharding import PartitionSpec as P

PIXEL_CHUNK = 1024
LOW_COLUMNS = 256
MIB = 1024 * 1024

F32 = jnp.float32
BF16 = jnp.bfloat16
SMEM = pl.BlockSpec(memory_space=pltpu.SMEM)
VMEM = pl.BlockSpec(memory_space=pltpu.VMEM)
ANY = pl.BlockSpec(memory_space=pl.ANY)
WIDE_PARAMS = pltpu.CompilerParams(vmem_limit_bytes=60 * MIB)
PARAMS = pltpu.CompilerParams(vmem_limit_bytes=24 * MIB)

EARLY = (6, 1, 7)
LATE = (2, 3, 5, 4)


def cost(flops, bytes_accessed):
    return pl.CostEstimate(flops=int(flops), bytes_accessed=int(bytes_accessed), transcendentals=0)


def place_and_band(splits):
    count = lax.axis_size("sim")
    bands = count // splits
    device = lax.axis_index("sim")
    logical = lax.rem(device + (count - bands // 2), count)
    return lax.div(device, bands), lax.rem(logical, bands)


def slot_at(place, d, tiles, depth):
    slot = lax.bitwise_xor(place, d)
    block = lax.div(slot, tiles)
    half = lax.bitwise_and(lax.bitwise_xor(block, lax.div(block, 2)), 1)
    return half, pl.multiple_of(lax.div(block, 2) * depth, depth), lax.rem(slot, tiles)


def keep_kernel(rows, width, a_ref, b_ref, *refs):
    keep_ref, total = refs[-2:]
    pixels = a_ref.shape[1]
    tall = total.shape[0]
    total[...] = jnp.zeros_like(total)

    @pl.loop(0, pixels // PIXEL_CHUNK)
    def _(step):
        part = pl.ds(pl.multiple_of(step * PIXEL_CHUNK, PIXEL_CHUNK), PIXEL_CHUNK)
        high = lax.broadcasted_iota(jnp.int32, (tall, PIXEL_CHUNK), 0) == a_ref[:, part]
        low = lax.broadcasted_iota(jnp.int32, (LOW_COLUMNS, PIXEL_CHUNK), 0) == b_ref[:, part]
        total[...] += lax.dot_general(
            high.astype(F32).astype(BF16),
            low.astype(F32).astype(BF16),
            (((1,), (1,)), ((), ())),
            preferred_element_type=F32,
        )

    per_tile = width // LOW_COLUMNS
    for block in range(tall // rows):
        tile, piece = block // per_tile, block % per_tile
        count = total[block * rows : (block + 1) * rows, :]
        keep_ref[tile, :, piece * LOW_COLUMNS : (piece + 1) * LOW_COLUMNS] = jnp.where(
            count > 0, 0.0, 1.0
        ).astype(BF16)


def keep_mask(source_pixels, band_index, rows, columns, width, after):
    offsets = source_pixels - band_index * rows * columns
    inside = (offsets >= 0) & (offsets < rows * columns)
    row, column = offsets // columns, offsets % columns
    a = jnp.where(inside, (column // LOW_COLUMNS) * rows + row, -1)
    b = column % LOW_COLUMNS
    pixels = source_pixels.shape[0]
    extra = -pixels % PIXEL_CHUNK
    a = jnp.pad(a, (0, extra), constant_values=-1)[None]
    b = jnp.pad(b, (0, extra))[None]
    tall = columns // LOW_COLUMNS * rows
    return pl.pallas_call(
        functools.partial(keep_kernel, rows, width),
        out_shape=jax.ShapeDtypeStruct((columns // width, rows, width), BF16),
        in_specs=[VMEM, VMEM] + [ANY] * len(after),
        out_specs=VMEM,
        scratch_shapes=[pltpu.VMEM((tall, LOW_COLUMNS), F32)],
        compiler_params=PARAMS,
        cost_estimate=cost(2 * tall * LOW_COLUMNS * (pixels + extra), 4 * rows * columns),
        name="keep",
    )(a, b, *after)


def rim_sides(splits, band):
    if lax.axis_size("sim") // splits == 2:
        return [band == 0]
    return [False, True]


def as_rows(values, rows, width):
    values = values + [jnp.zeros((rows - len(values), width), F32)]
    return jnp.concatenate(values, axis=0).astype(BF16)


def wiener_kernel(splits, index_ref, share_ref, sky_ref, sim_ref, matrix_ref, out_ref, *refs):
    scale_ref, edge_refs, (held, sems) = refs[0], refs[1:-2], refs[-2:]
    fields, tiles, rows, width = out_ref.shape
    copies = [pltpu.make_async_copy(sky_ref, held.at[0], sems.at[0])]
    for field in range(1, fields):
        source = sim_ref.at[index_ref[field - 1]]
        copies.append(pltpu.make_async_copy(source, held.at[field], sems.at[field]))
    for copy in copies:
        copy.start()
    for copy in copies:
        copy.wait()
    for tile in range(tiles):
        values = held[:, :, tile * width : (tile + 1) * width].reshape(fields * rows, width)
        result = jnp.dot(values, matrix_ref[...], preferred_element_type=F32).astype(BF16)
        out_ref[:, tile] = result.reshape(fields, rows, width)
    for field in range(fields):
        scale_ref[field : field + 1, :] = jnp.full((1, scale_ref.shape[1]), share_ref[field], F32)
    _, band = place_and_band(splits)
    for upper, edge_ref in zip(rim_sides(splits, band), edge_refs):
        for tile in range(tiles):
            picked = []
            for field in range(fields):
                low = out_ref[field, tile, :16, :].astype(F32)[:1]
                high = out_ref[field, tile, rows - 16 :, :].astype(F32)[15:]
                picked.append(jnp.where(upper, high, low) * share_ref[field])
            columns = pl.ds(tile * width, width)
            edge_ref[:, columns] = as_rows(picked, edge_ref.shape[0], width)


def rim_shapes(splits, fields, columns):
    count = 1 if lax.axis_size("sim") // splits == 2 else 2
    return [jax.ShapeDtypeStruct((-(-(fields + 1) // 8) * 8, columns), BF16)] * count


def wiener_fields(splits, sim_index, shares, sky_maps, sim_sky, matrix):
    rows, columns = sky_maps.shape
    width = matrix.shape[0]
    fields = sim_index.shape[0] + 1
    rims = rim_shapes(splits, fields, columns)
    wiener, scale, *edge = pl.pallas_call(
        functools.partial(wiener_kernel, splits),
        out_shape=[
            jax.ShapeDtypeStruct((fields, columns // width, rows, width), BF16),
            jax.ShapeDtypeStruct((-(-fields // 8) * 8, 128), F32),
            *rims,
        ],
        in_specs=[SMEM, SMEM, ANY, ANY, VMEM],
        out_specs=[VMEM] * (2 + len(rims)),
        scratch_shapes=[
            pltpu.VMEM((fields, rows, columns), BF16),
            pltpu.SemaphoreType.DMA((fields,)),
        ],
        compiler_params=PARAMS,
        cost_estimate=cost(2 * fields * rows * columns * width, 4 * fields * rows * columns),
        name="wiener",
    )(sim_index, shares, sky_maps, sim_sky, matrix)
    return wiener, scale, edge


def pack_kernel(splits, order, index_ref, ivf_ref, sim_ref, *refs):
    outs, held, sems = refs[: len(order)], refs[-2], refs[-1]
    fields, depth, width = outs[0].shape
    rows, columns = ivf_ref.shape
    place, _ = place_and_band(splits)

    def region(d):
        half, row, tile = slot_at(place, d, columns // width, depth)
        part = pl.ds(pl.multiple_of(half * (rows // 2) + row, depth), depth)
        return part, pl.ds(pl.multiple_of(tile * width, width), width)

    alone = len(order) == 1
    wanted = region(order[0]) if alone else (slice(None), slice(None))
    copies = [pltpu.make_async_copy(ivf_ref.at[wanted], held.at[0], sems.at[0])]
    for field in range(1, fields):
        source = sim_ref.at[(index_ref[field - 1],) + wanted]
        copies.append(pltpu.make_async_copy(source, held.at[field], sems.at[field]))
    for copy in copies:
        copy.start()
    for field in range(fields):
        copies[field].wait()
        for d, out in zip(order, outs):
            out[field] = held[field] if alone else held[(field,) + region(d)]


def pack(splits, order, sim_index, ivf_maps, sim_ivf, depth, width):
    fields = sim_index.shape[0] + 1
    held = (depth, width) if len(order) == 1 else ivf_maps.shape
    chunks = pl.pallas_call(
        functools.partial(pack_kernel, splits, order),
        out_shape=[jax.ShapeDtypeStruct((fields, depth, width), BF16)] * len(order),
        in_specs=[SMEM, ANY, ANY],
        out_specs=[VMEM] * len(order),
        scratch_shapes=[
            pltpu.VMEM((fields,) + held, BF16),
            pltpu.SemaphoreType.DMA((fields,)),
        ],
        compiler_params=WIDE_PARAMS,
        cost_estimate=cost(0, 4 * len(order) * fields * depth * width),
        name="pack",
    )(sim_index, ivf_maps, sim_ivf)
    return dict(zip(order, chunks))


def prepare_kernel(splits, pair_ref, own_ref, weights_ref, held_ref, sem):
    copy = pltpu.make_async_copy(own_ref, held_ref, sem)
    copy.start()
    size = weights_ref.shape[0]
    depth = size // splits
    place, band = place_and_band(splits)
    bands = lax.axis_size("sim") // splits
    shift = (band >= bands - bands // 2).astype(jnp.int32)
    split_of = [lax.rem(lax.bitwise_xor(place, d) + splits - shift, splits) for d in range(splits)]
    row = lax.broadcasted_iota(jnp.int32, (size, size), 0)
    column = lax.broadcasted_iota(jnp.int32, (size, size), 1)
    total = jnp.zeros((size, size), F32)
    for d in range(splits):
        for e in range(splits):
            if d != e:
                here = (lax.div(row, depth) == d) & (lax.div(column, depth) == e)
                value = pair_ref[split_of[d], split_of[e]].astype(F32)
                total = jnp.where(here, value, total)
    same = lax.rem(row, depth) == lax.rem(column, depth)
    weights_ref[...] = jnp.where(same, total, 0.0).astype(BF16)
    copy.wait()


def prepare(pair_table, own):
    splits = pair_table.shape[0]
    size = splits * own.shape[1]
    return pl.pallas_call(
        functools.partial(prepare_kernel, splits),
        out_shape=[
            jax.ShapeDtypeStruct((size, size), BF16),
            jax.ShapeDtypeStruct(own.shape, BF16),
        ],
        in_specs=[SMEM, ANY],
        out_specs=[VMEM, VMEM],
        scratch_shapes=[pltpu.SemaphoreType.DMA],
        compiler_params=PARAMS,
        cost_estimate=cost(splits * splits * size * size, 4 * own.size),
        name="prepare",
    )(pair_table, own)


def mix_kernel(order, weights_ref, *refs):
    parts = len(order)
    chunks, outs = refs[:parts], refs[parts:]
    fields, depth, _ = chunks[0].shape
    for field in range(fields):
        stacked = jnp.concatenate([chunks[order.index(d)][field] for d in range(parts)], axis=0)
        mixed = jnp.dot(weights_ref[...], stacked, preferred_element_type=F32).astype(BF16)
        for d in range(parts):
            outs[d][field] = mixed[d * depth : (d + 1) * depth]


def mix(weights, chunks):
    order = EARLY + LATE + (0,)
    parts = len(chunks)
    shape = chunks[0].shape
    size = shape[0] * shape[1] * shape[2]
    return pl.pallas_call(
        functools.partial(mix_kernel, order),
        out_shape=[jax.ShapeDtypeStruct(shape, BF16)] * parts,
        in_specs=[VMEM] * (parts + 1),
        out_specs=[VMEM] * parts,
        compiler_params=PARAMS,
        cost_estimate=cost(2 * parts * size * weights.shape[0], 4 * parts * size),
        name="mix",
    )(weights, *[chunks[d] for d in order])


def half_kernel(
    splits, order, late, keep_ref, wiener_ref, scale_ref, matrix_ref, response_ref, *refs
):
    chunks = refs[: len(order)]
    fields, depth, width = chunks[0].shape
    if late:
        early_sums_ref, early_dec_ref = refs[len(order) : len(order) + 2]
        part_ref, dec_ref, sums_ref, grad_ref, ra_ref = refs[len(order) + 2 :]
    else:
        sums_ref, part_ref, early_dec_ref, grad_ref, ra_ref = refs[len(order) :]
    tiles, rows = sums_ref.shape[1:3]
    place, band = place_and_band(splits)
    half = slot_at(place, order[0], tiles, depth)[0]
    here = pl.ds(pl.multiple_of(half * rows, rows), rows)
    other = pl.ds(pl.multiple_of((1 - half) * rows, rows), rows)
    for d, chunk in zip(order, chunks):
        _, row, tile = slot_at(place, d, tiles, depth)
        there = pl.ds(pl.multiple_of(half * rows + row, depth), depth)
        keep = keep_ref[tile, there, :]
        for field in range(fields):
            sums_ref[field, tile, pl.ds(row, depth), :] = chunk[field] * keep
    grad_ref[...] = jnp.dot(
        sums_ref[...].reshape(fields * tiles * rows, width),
        matrix_ref[...],
        preferred_element_type=F32,
    ).reshape(grad_ref.shape)
    response = response_ref[pl.ds(pl.multiple_of((2 * band + half) * rows, rows), rows), :]
    line = lax.broadcasted_iota(jnp.int32, (rows, width), 0)
    sources = []
    for tile in range(tiles):
        ra = dec = src = first = last = 0.0
        for field in range(fields):
            wide = sums_ref[field, tile].astype(F32)
            share = scale_ref[field : field + 1, :1]
            weight = wiener_ref[field, tile, here, :].astype(F32) * share
            above, below = pltpu.roll(wide, rows - 1, 0), pltpu.roll(wide, 1, 0)
            above_fill = below_fill = 0.0
            if late:
                near = early_sums_ref[field, tile].astype(F32)
                above_fill = jnp.where(half == 0, near[:1], 0.0)
                below_fill = jnp.where(half == 1, near[rows - 1 :], 0.0)
                beside = wiener_ref[field, tile, other, :].astype(F32) * share
                last = last + 0.5 * beside[rows - 1 :] * wide[:1]
                first = first - 0.5 * beside[:1] * wide[rows - 1 :]
            above = jnp.where(line == rows - 1, above_fill, above)
            below = jnp.where(line == 0, below_fill, below)
            ra = ra + weight * grad_ref[field, tile]
            dec = dec + weight * ((above - below) * 0.5)
            src = src + weight * wide
        high = ra.astype(BF16)
        ra_ref[tile, 0] = high
        ra_ref[tile, 1] = (ra - high.astype(F32)).astype(BF16)
        sources.append(response * src)
        if late:
            early_dec = early_dec_ref[tile]
            early_dec = early_dec + jnp.where((line == rows - 1) & (half == 1), last, 0.0)
            early_dec = early_dec + jnp.where((line == 0) & (half == 0), first, 0.0)
            dec_ref[tile, here, :] = dec
            dec_ref[tile, other, :] = early_dec
        else:
            early_dec_ref[tile] = dec
    both = jnp.dot(
        ra_ref[...].reshape(tiles * 2 * rows, width), matrix_ref[...], preferred_element_type=F32
    ).reshape(tiles, 2, rows, width)
    for tile in range(tiles):
        part_ref[tile] = -(both[tile, 0] + both[tile, 1]) - sources[tile]


def half_call(splits, order, keep, wiener, scale, matrix, response, chunks, early):
    fields, depth, width = chunks[0].shape
    tiles, all_rows, _ = keep.shape
    rows = all_rows // 2
    late = early is not None
    sums = (fields, tiles, rows, width)
    scratch = [pltpu.VMEM(sums, F32), pltpu.VMEM((tiles, 2, rows, width), BF16)]
    part = jax.ShapeDtypeStruct((tiles, rows, width), F32)
    if late:
        out_shape = [part, jax.ShapeDtypeStruct((tiles, all_rows, width), F32)]
        scratch = [pltpu.VMEM(sums, BF16)] + scratch
    else:
        out_shape = [jax.ShapeDtypeStruct(sums, BF16), part, part]
    operands = [keep, wiener, scale, matrix, response, *chunks, *(early or [])]
    return pl.pallas_call(
        functools.partial(half_kernel, splits, order, late),
        out_shape=out_shape,
        in_specs=[VMEM] * len(operands),
        out_specs=[VMEM] * len(out_shape),
        scratch_shapes=scratch,
        compiler_params=PARAMS,
        cost_estimate=cost(2 * (fields + 2) * tiles * rows * width * width, 16 * tiles * rows * width),
        name="late_half" if late else "early_half",
    )(*operands)


def slope(values):
    rows = values.shape[0]
    line = lax.broadcasted_iota(jnp.int32, values.shape, 0)
    above = jnp.where(line == rows - 1, 0.0, pltpu.roll(values, rows - 1, 0))
    below = jnp.where(line == 0, 0.0, pltpu.roll(values, 1, 0))
    return (above - below) * 0.5


def edges_kernel(splits, order, keep_ref, *refs):
    place, band = place_and_band(splits)
    sides = rim_sides(splits, band)
    weights, chunks = refs[: len(sides)], refs[len(sides) : len(sides) + splits]
    outs, (block, outermost, inner) = refs[-3 - len(sides) : -3], refs[-3:]
    fields, depth, width = chunks[0].shape
    tiles, rows, _ = keep_ref.shape
    outermost[...] = jnp.zeros_like(outermost)
    inner[...] = jnp.zeros_like(inner)
    for upper, weight_ref, out_ref in zip(sides, weights, outs):
        edge_row = jnp.where(upper, rows - depth, 0)
        there = pl.ds(pl.multiple_of(edge_row, depth), depth)
        for d, chunk in zip(order, chunks):
            half, row, tile = slot_at(place, d, tiles, depth)

            @pl.when(half * (rows // 2) + row == edge_row)
            def _():
                keep = keep_ref[tile, there, :]
                for field in range(fields):
                    block[...] = (chunk[field] * keep).astype(F32)
                    last = jnp.where(upper, depth - 1, 0)
                    outermost[field : field + 1, :] = block[pl.ds(last, 1), :]
                    inner[field : field + 1, :] = block[pl.ds(jnp.where(upper, depth - 2, 1), 1), :]
                columns = pl.ds(pl.multiple_of(tile * width, width), width)
                beyond = weight_ref[:, columns].astype(F32) * inner[...]
                outermost[fields : fields + 1, :] = jnp.sum(beyond, axis=0, keepdims=True)
                out_ref[:, columns] = outermost[...].astype(BF16)


def edges(splits, order, keep, w_edge, chunks, after):
    fields, depth, width = chunks[0].shape
    rims = rim_shapes(splits, fields, keep.shape[0] * width)
    rows = rims[0].shape[0]
    return pl.pallas_call(
        functools.partial(edges_kernel, splits, order),
        out_shape=rims,
        in_specs=[VMEM] * (splits + 1 + len(rims)) + [ANY] * len(after),
        out_specs=[VMEM] * len(rims),
        scratch_shapes=[
            pltpu.VMEM((depth, width), F32),
            pltpu.VMEM((rows, width), F32),
            pltpu.VMEM((rows, width), F32),
        ],
        compiler_params=PARAMS,
        cost_estimate=cost(0, 2 * splits * fields * depth * width),
        name="edges",
    )(keep, *w_edge, *chunks, *after)


def finish_kernel(splits, fields, early_ref, late_ref, dec_ref, *refs):
    rims, (out_ref, sums) = refs[:-2], refs[-2:]
    tiles, rows, width = dec_ref.shape
    half_rows = rows // 2
    place, band = place_and_band(splits)
    bands = lax.axis_size("sim") // splits
    half = slot_at(place, 0, tiles, rows * tiles // splits)[0]
    here = pl.ds(pl.multiple_of(half * half_rows, half_rows), half_rows)
    other = pl.ds(pl.multiple_of((1 - half) * half_rows, half_rows), half_rows)
    line = lax.broadcasted_iota(jnp.int32, (8, 1), 0)
    sides = [(band > 0, band == 0)] if bands == 2 else [(band > 0, False), (False, band < bands - 1)]
    for tile in range(tiles):
        sums[tile, here, :] = early_ref[tile]
        sums[tile, other, :] = late_ref[tile]
        sums[tile] = sums[tile] - slope(dec_ref[tile])
        columns = pl.ds(tile * width, width)
        for number, (low, high) in enumerate(sides):
            own_w, far_w, own, far = [
                ref[:, columns].astype(F32) for ref in rims[4 * number : 4 * number + 4]
            ]
            inner = 0.25 * jnp.sum(own_w * far, axis=0, keepdims=True)
            outer = jnp.sum(far_w * own, axis=0, keepdims=True) - far[fields : fields + 1]
            outer = 0.25 * outer
            first, last = sums[tile, :8, :], sums[tile, rows - 8 :, :]
            first += jnp.where((line == 0) & low, outer, 0.0)
            first -= jnp.where((line == 1) & low, inner, 0.0)
            last += jnp.where((line == 7) & high, outer, 0.0)
            last -= jnp.where((line == 6) & high, inner, 0.0)
            sums[tile, :8, :] = first
            sums[tile, rows - 8 :, :] = last
        out_ref[:, columns] = sums[tile]


def finish(splits, fields, early_part, late_part, dec, rims):
    tiles, rows, width = dec.shape
    return pl.pallas_call(
        functools.partial(finish_kernel, splits, fields),
        out_shape=pltpu.HBM((rows, tiles * width), F32),
        in_specs=[VMEM] * (3 + len(rims)),
        out_specs=VMEM,
        scratch_shapes=[pltpu.VMEM((tiles, rows, width), F32)],
        compiler_params=PARAMS,
        cost_estimate=cost(0, 12 * tiles * rows * width),
        name="finish",
    )(early_part, late_part, dec, *rims)


def distinct_kernel(index_ref, count_ref, distinct_ref, share_ref):
    uses = index_ref.shape[0]
    share_ref[0] = jnp.float32(1.0)
    for number in range(uses):
        distinct_ref[number] = index_ref[0]
        share_ref[number + 1] = jnp.float32(0.0)
    count = jnp.int32(0)
    for number in range(uses):
        same = [(index_ref[other] == index_ref[number]).astype(jnp.int32) for other in range(uses)]
        new = sum(same[:number], jnp.int32(0)) == 0
        times = sum(same, jnp.int32(0)).astype(F32)

        @pl.when(new)
        def _():
            distinct_ref[count] = index_ref[number]
            share_ref[count + 1] = times * (-1.0 / uses)

        count = count + new.astype(jnp.int32)
    count_ref[0] = count


def distinct_fields(sim_index):
    uses = sim_index.shape[0]
    return pl.pallas_call(
        distinct_kernel,
        out_shape=[
            jax.ShapeDtypeStruct((1,), jnp.int32),
            jax.ShapeDtypeStruct((uses,), jnp.int32),
            jax.ShapeDtypeStruct((uses + 1,), F32),
        ],
        in_specs=[SMEM],
        out_specs=[SMEM] * 3,
        name="distinct",
    )(sim_index)


def estimate(
    sky_maps,
    ivf_maps,
    sim_sky,
    sim_ivf,
    ra_wiener,
    ra_gradient,
    pair_table,
    sim_index,
    shares,
    source_pixels,
    response,
):
    splits = pair_table.shape[0]
    axis_count = lax.axis_size("sim")
    bands = axis_count // splits
    place, band = place_and_band(splits)
    rows, columns = sky_maps.shape
    width = ra_gradient.shape[0]
    depth = rows * (columns // width) // splits

    def swap(block, d):
        pairs = [
            (g * bands + u, (g ^ d) * bands + u) for g in range(splits) for u in range(bands)
        ]
        return lax.ppermute(block, "sim", pairs)

    def exchange(blocks):
        moved = {d: swap(blocks[d], d) for d in EARLY + LATE}
        return {0: blocks[0], **moved}

    def neighbours(edge):
        if bands == 2:
            pairs = [((k + 1) % axis_count, k) if k % 2 else ((k - 1) % axis_count, k)
                     for k in range(axis_count)]
            return [edge[0], lax.ppermute(edge[0], "sim", pairs)]
        ahead = [(k, (k + 1) % axis_count) for k in range(axis_count)]
        back = [((k + 1) % axis_count, k) for k in range(axis_count)]
        below, above = lax.ppermute(edge[1], "sim", ahead), lax.ppermute(edge[0], "sim", back)
        return [edge[0], below, edge[1], above]

    first, rest = EARLY[:1], (0,) + EARLY[1:] + LATE
    sent = pack(splits, first, sim_index, ivf_maps, sim_ivf, depth, width)
    sent.update(pack(splits, rest, sim_index, ivf_maps, sim_ivf, depth, width))
    arrived = exchange(sent)
    wiener, scale, w_edge = wiener_fields(splits, sim_index, shares, sky_maps, sim_sky, ra_wiener)
    w_rims = neighbours(w_edge)
    keep = keep_mask(source_pixels, band, rows, columns, width, [])
    weights, arrived[0] = prepare(pair_table, arrived[0])
    sums = exchange(mix(weights, arrived))
    shared = keep, wiener, scale, ra_gradient, response[:, None]
    early, late = (0,) + EARLY, LATE
    early_results = half_call(splits, early, *shared, [sums[d] for d in early], None)
    order = early + late
    edge = edges(splits, order, keep, w_edge, [sums[d] for d in order], early_results[1:2])
    s_rims = neighbours(edge)
    rims = [rim for n in range(0, len(s_rims), 2) for rim in w_rims[n : n + 2] + s_rims[n : n + 2]]
    late_part, dec = half_call(
        splits, late, *shared, [sums[d] for d in late], early_results[::2]
    )
    return finish(splits, shares.shape[0], early_results[1], late_part, dec, rims)


def on_device(
    sky_maps,
    ivf_maps,
    sim_sky,
    sim_ivf,
    ra_wiener,
    ra_gradient,
    pair_table,
    sim_index,
    source_pixels,
    response,
):
    uses = sim_index.shape[0]
    count, distinct, shares = distinct_fields(sim_index)
    sizes = range(max(1, uses - 2), uses + 1)

    def of_size(size):
        def run(distinct, shares):
            return estimate(
                sky_maps,
                ivf_maps,
                sim_sky,
                sim_ivf,
                ra_wiener,
                ra_gradient,
                pair_table,
                distinct[:size],
                shares[: size + 1],
                source_pixels,
                response,
            )

        return run

    branch = jnp.clip(count[0] - sizes[0], 0, len(sizes) - 1)
    return lax.switch(branch, [of_size(size) for size in sizes], distinct, shares)


def solution(mesh):
    in_specs = (
        P(("patch", "sim"), None),
        P(("patch", "sim"), None),
        P(None, ("patch", "sim"), None),
        P(None, ("patch", "sim"), None),
        P(),
        P(),
        P(),
        P(),
        P("patch"),
        P("patch"),
    )
    out_specs = P(("patch", "sim"), None)
    return jax.shard_map(
        on_device, mesh=mesh, in_specs=in_specs, out_specs=out_specs, check_vma=False
    )
```

```python
import functools

import jax
import jax.numpy as jnp
from jax import lax
from jax.experimental import pallas as pl
from jax.experimental.pallas import tpu as pltpu
from jax.sharding import PartitionSpec as P

PIXEL_CHUNK = 1024
LOW_COLUMNS = 256
MIB = 1024 * 1024

F32 = jnp.float32
BF16 = jnp.bfloat16
SMEM = pl.BlockSpec(memory_space=pltpu.SMEM)
VMEM = pl.BlockSpec(memory_space=pltpu.VMEM)
ANY = pl.BlockSpec(memory_space=pl.ANY)
WIDE_PARAMS = pltpu.CompilerParams(vmem_limit_bytes=60 * MIB)
PARAMS = pltpu.CompilerParams(vmem_limit_bytes=24 * MIB)

EARLY = (6, 1, 7)
LATE = (2, 3, 5, 4)


def cost(flops, bytes_accessed):
    return pl.CostEstimate(flops=int(flops), bytes_accessed=int(bytes_accessed), transcendentals=0)


def place_and_band(splits):
    count = lax.axis_size("sim")
    bands = count // splits
    device = lax.axis_index("sim")
    logical = lax.rem(device + (count - bands // 2), count)
    return lax.div(device, bands), lax.rem(logical, bands)


def slot_at(place, d, tiles, depth):
    slot = lax.bitwise_xor(place, d)
    block = lax.div(slot, tiles)
    half = lax.bitwise_and(lax.bitwise_xor(block, lax.div(block, 2)), 1)
    return half, pl.multiple_of(lax.div(block, 2) * depth, depth), lax.rem(slot, tiles)


def keep_kernel(rows, width, a_ref, b_ref, *refs):
    keep_ref, total = refs[-2:]
    pixels = a_ref.shape[1]
    tall = total.shape[0]
    total[...] = jnp.zeros_like(total)

    @pl.loop(0, pixels // PIXEL_CHUNK)
    def _(step):
        part = pl.ds(pl.multiple_of(step * PIXEL_CHUNK, PIXEL_CHUNK), PIXEL_CHUNK)
        high = lax.broadcasted_iota(jnp.int32, (tall, PIXEL_CHUNK), 0) == a_ref[:, part]
        low = lax.broadcasted_iota(jnp.int32, (LOW_COLUMNS, PIXEL_CHUNK), 0) == b_ref[:, part]
        total[...] += lax.dot_general(
            high.astype(F32).astype(BF16),
            low.astype(F32).astype(BF16),
            (((1,), (1,)), ((), ())),
            preferred_element_type=F32,
        )

    per_tile = width // LOW_COLUMNS
    for block in range(tall // rows):
        tile, piece = block // per_tile, block % per_tile
        count = total[block * rows : (block + 1) * rows, :]
        keep_ref[tile, :, piece * LOW_COLUMNS : (piece + 1) * LOW_COLUMNS] = jnp.where(
            count > 0, 0.0, 1.0
        ).astype(BF16)


def keep_mask(source_pixels, band_index, rows, columns, width, after):
    offsets = source_pixels - band_index * rows * columns
    inside = (offsets >= 0) & (offsets < rows * columns)
    row, column = offsets // columns, offsets % columns
    a = jnp.where(inside, (column // LOW_COLUMNS) * rows + row, -1)
    b = column % LOW_COLUMNS
    pixels = source_pixels.shape[0]
    extra = -pixels % PIXEL_CHUNK
    a = jnp.pad(a, (0, extra), constant_values=-1)[None]
    b = jnp.pad(b, (0, extra))[None]
    tall = columns // LOW_COLUMNS * rows
    return pl.pallas_call(
        functools.partial(keep_kernel, rows, width),
        out_shape=jax.ShapeDtypeStruct((columns // width, rows, width), BF16),
        in_specs=[VMEM, VMEM] + [ANY] * len(after),
        out_specs=VMEM,
        scratch_shapes=[pltpu.VMEM((tall, LOW_COLUMNS), F32)],
        compiler_params=PARAMS,
        cost_estimate=cost(2 * tall * LOW_COLUMNS * (pixels + extra), 4 * rows * columns),
        name="keep",
    )(a, b, *after)


def rim_sides(splits, band):
    if lax.axis_size("sim") // splits == 2:
        return [band == 0]
    return [False, True]


def as_rows(values, rows, width):
    values = values + [jnp.zeros((rows - len(values), width), F32)]
    return jnp.concatenate(values, axis=0).astype(BF16)


def wiener_kernel(splits, index_ref, share_ref, sky_ref, sim_ref, matrix_ref, out_ref, *refs):
    scale_ref, edge_refs, (held, sems) = refs[0], refs[1:-2], refs[-2:]
    fields, tiles, rows, width = out_ref.shape
    copies = [pltpu.make_async_copy(sky_ref, held.at[0], sems.at[0])]
    for field in range(1, fields):
        source = sim_ref.at[index_ref[field - 1]]
        copies.append(pltpu.make_async_copy(source, held.at[field], sems.at[field]))
    for copy in copies:
        copy.start()
    for copy in copies:
        copy.wait()
    for tile in range(tiles):
        values = held[:, :, tile * width : (tile + 1) * width].reshape(fields * rows, width)
        result = jnp.dot(values, matrix_ref[...], preferred_element_type=F32).astype(BF16)
        out_ref[:, tile] = result.reshape(fields, rows, width)
    for field in range(fields):
        scale_ref[field : field + 1, :] = jnp.full((1, scale_ref.shape[1]), share_ref[field], F32)
    _, band = place_and_band(splits)
    for upper, edge_ref in zip(rim_sides(splits, band), edge_refs):
        for tile in range(tiles):
            picked = []
            for field in range(fields):
                low = out_ref[field, tile, :16, :].astype(F32)[:1]
                high = out_ref[field, tile, rows - 16 :, :].astype(F32)[15:]
                picked.append(jnp.where(upper, high, low) * share_ref[field])
            columns = pl.ds(tile * width, width)
            edge_ref[:, columns] = as_rows(picked, edge_ref.shape[0], width)


def rim_shapes(splits, fields, columns):
    count = 1 if lax.axis_size("sim") // splits == 2 else 2
    return [jax.ShapeDtypeStruct((-(-(fields + 1) // 8) * 8, columns), BF16)] * count


def wiener_fields(splits, sim_index, shares, sky_maps, sim_sky, matrix):
    rows, columns = sky_maps.shape
    width = matrix.shape[0]
    fields = sim_index.shape[0] + 1
    rims = rim_shapes(splits, fields, columns)
    wiener, scale, *edge = pl.pallas_call(
        functools.partial(wiener_kernel, splits),
        out_shape=[
            jax.ShapeDtypeStruct((fields, columns // width, rows, width), BF16),
            jax.ShapeDtypeStruct((-(-fields // 8) * 8, 128), F32),
            *rims,
        ],
        in_specs=[SMEM, SMEM, ANY, ANY, VMEM],
        out_specs=[VMEM] * (2 + len(rims)),
        scratch_shapes=[
            pltpu.VMEM((fields, rows, columns), BF16),
            pltpu.SemaphoreType.DMA((fields,)),
        ],
        compiler_params=PARAMS,
        cost_estimate=cost(2 * fields * rows * columns * width, 4 * fields * rows * columns),
        name="wiener",
    )(sim_index, shares, sky_maps, sim_sky, matrix)
    return wiener, scale, edge


def region(place, d, rows, columns, depth, width):
    half, row, tile = slot_at(place, d, columns // width, depth)
    part = pl.ds(pl.multiple_of(half * (rows // 2) + row, depth), depth)
    return part, pl.ds(pl.multiple_of(tile * width, width), width)


def pack_kernel(splits, order, index_ref, ivf_ref, sim_ref, *refs):
    outs, held, sems = refs[-2 - len(order) : -2], refs[-2], refs[-1]
    fields, depth, width = outs[0].shape
    rows, columns = ivf_ref.shape
    place, _ = place_and_band(splits)
    copies = [pltpu.make_async_copy(ivf_ref, held.at[0], sems.at[0])]
    for field in range(1, fields):
        source = sim_ref.at[index_ref[field - 1]]
        copies.append(pltpu.make_async_copy(source, held.at[field], sems.at[field]))
    for copy in copies:
        copy.start()
    for field in range(fields):
        copies[field].wait()
        for d, out in zip(order, outs):
            out[field] = held[(field,) + region(place, d, rows, columns, depth, width)]


def pack(splits, order, sim_index, ivf_maps, sim_ivf, depth, width, after):
    fields = sim_index.shape[0] + 1
    chunks = pl.pallas_call(
        functools.partial(pack_kernel, splits, order),
        out_shape=[jax.ShapeDtypeStruct((fields, depth, width), BF16)] * len(order),
        in_specs=[SMEM, ANY, ANY] + [ANY] * len(after),
        out_specs=[VMEM] * len(order),
        scratch_shapes=[
            pltpu.VMEM((fields,) + ivf_maps.shape, BF16),
            pltpu.SemaphoreType.DMA((fields,)),
        ],
        compiler_params=WIDE_PARAMS,
        cost_estimate=cost(0, 4 * len(order) * fields * depth * width),
        name="pack",
    )(sim_index, ivf_maps, sim_ivf, *after)
    return dict(zip(order, chunks))


def prepare_kernel(splits, pair_ref, own_ref, weights_ref, held_ref, sem):
    copy = pltpu.make_async_copy(own_ref, held_ref, sem)
    copy.start()
    size = weights_ref.shape[0]
    depth = size // splits
    place, band = place_and_band(splits)
    bands = lax.axis_size("sim") // splits
    shift = (band >= bands - bands // 2).astype(jnp.int32)
    split_of = [lax.rem(lax.bitwise_xor(place, d) + splits - shift, splits) for d in range(splits)]
    row = lax.broadcasted_iota(jnp.int32, (size, size), 0)
    column = lax.broadcasted_iota(jnp.int32, (size, size), 1)
    total = jnp.zeros((size, size), F32)
    for d in range(splits):
        for e in range(splits):
            if d != e:
                here = (lax.div(row, depth) == d) & (lax.div(column, depth) == e)
                value = pair_ref[split_of[d], split_of[e]].astype(F32)
                total = jnp.where(here, value, total)
    same = lax.rem(row, depth) == lax.rem(column, depth)
    weights_ref[...] = jnp.where(same, total, 0.0).astype(BF16)
    copy.wait()


def prepare(pair_table, own):
    splits = pair_table.shape[0]
    size = splits * own.shape[1]
    return pl.pallas_call(
        functools.partial(prepare_kernel, splits),
        out_shape=[
            jax.ShapeDtypeStruct((size, size), BF16),
            jax.ShapeDtypeStruct(own.shape, BF16),
        ],
        in_specs=[SMEM, ANY],
        out_specs=[VMEM, VMEM],
        scratch_shapes=[pltpu.SemaphoreType.DMA],
        compiler_params=PARAMS,
        cost_estimate=cost(splits * splits * size * size, 4 * own.size),
        name="prepare",
    )(pair_table, own)


def mix_kernel(order, weights_ref, *refs):
    parts = len(order)
    chunks, outs = refs[:parts], refs[parts:]
    fields, depth, _ = chunks[0].shape
    for field in range(fields):
        stacked = jnp.concatenate([chunks[order.index(d)][field] for d in range(parts)], axis=0)
        mixed = jnp.dot(weights_ref[...], stacked, preferred_element_type=F32).astype(BF16)
        for d in range(parts):
            outs[d][field] = mixed[d * depth : (d + 1) * depth]


def mix(weights, chunks):
    order = EARLY + LATE + (0,)
    parts = len(chunks)
    shape = chunks[0].shape
    size = shape[0] * shape[1] * shape[2]
    return pl.pallas_call(
        functools.partial(mix_kernel, order),
        out_shape=[jax.ShapeDtypeStruct(shape, BF16)] * parts,
        in_specs=[VMEM] * (parts + 1),
        out_specs=[VMEM] * parts,
        compiler_params=PARAMS,
        cost_estimate=cost(2 * parts * size * weights.shape[0], 4 * parts * size),
        name="mix",
    )(weights, *[chunks[d] for d in order])


def half_kernel(
    splits, order, late, keep_ref, wiener_ref, scale_ref, matrix_ref, response_ref, *refs
):
    chunks = refs[: len(order)]
    fields, depth, width = chunks[0].shape
    if late:
        early_sums_ref, early_dec_ref = refs[len(order) : len(order) + 2]
        part_ref, dec_ref, sums_ref, grad_ref, ra_ref = refs[len(order) + 2 :]
    else:
        sums_ref, part_ref, early_dec_ref, grad_ref, ra_ref = refs[len(order) :]
    tiles, rows = sums_ref.shape[1:3]
    place, band = place_and_band(splits)
    half = slot_at(place, order[0], tiles, depth)[0]
    here = pl.ds(pl.multiple_of(half * rows, rows), rows)
    other = pl.ds(pl.multiple_of((1 - half) * rows, rows), rows)
    for d, chunk in zip(order, chunks):
        _, row, tile = slot_at(place, d, tiles, depth)
        there = pl.ds(pl.multiple_of(half * rows + row, depth), depth)
        keep = keep_ref[tile, there, :]
        for field in range(fields):
            sums_ref[field, tile, pl.ds(row, depth), :] = chunk[field] * keep
    grad_ref[...] = jnp.dot(
        sums_ref[...].reshape(fields * tiles * rows, width),
        matrix_ref[...],
        preferred_element_type=F32,
    ).reshape(grad_ref.shape)
    response = response_ref[pl.ds(pl.multiple_of((2 * band + half) * rows, rows), rows), :]
    line = lax.broadcasted_iota(jnp.int32, (rows, width), 0)
    sources = []
    for tile in range(tiles):
        ra = dec = src = first = last = 0.0
        for field in range(fields):
            wide = sums_ref[field, tile].astype(F32)
            share = scale_ref[field : field + 1, :1]
            weight = wiener_ref[field, tile, here, :].astype(F32) * share
            above, below = pltpu.roll(wide, rows - 1, 0), pltpu.roll(wide, 1, 0)
            above_fill = below_fill = 0.0
            if late:
                near = early_sums_ref[field, tile].astype(F32)
                above_fill = jnp.where(half == 0, near[:1], 0.0)
                below_fill = jnp.where(half == 1, near[rows - 1 :], 0.0)
                beside = wiener_ref[field, tile, other, :].astype(F32) * share
                last = last + 0.5 * beside[rows - 1 :] * wide[:1]
                first = first - 0.5 * beside[:1] * wide[rows - 1 :]
            above = jnp.where(line == rows - 1, above_fill, above)
            below = jnp.where(line == 0, below_fill, below)
            ra = ra + weight * grad_ref[field, tile]
            dec = dec + weight * ((above - below) * 0.5)
            src = src + weight * wide
        high = ra.astype(BF16)
        ra_ref[tile, 0] = high
        ra_ref[tile, 1] = (ra - high.astype(F32)).astype(BF16)
        sources.append(response * src)
        if late:
            early_dec = early_dec_ref[tile]
            early_dec = early_dec + jnp.where((line == rows - 1) & (half == 1), last, 0.0)
            early_dec = early_dec + jnp.where((line == 0) & (half == 0), first, 0.0)
            dec_ref[tile, here, :] = dec
            dec_ref[tile, other, :] = early_dec
        else:
            early_dec_ref[tile] = dec
    both = jnp.dot(
        ra_ref[...].reshape(tiles * 2 * rows, width), matrix_ref[...], preferred_element_type=F32
    ).reshape(tiles, 2, rows, width)
    for tile in range(tiles):
        part_ref[tile] = -(both[tile, 0] + both[tile, 1]) - sources[tile]


def half_call(splits, order, keep, wiener, scale, matrix, response, chunks, early):
    fields, depth, width = chunks[0].shape
    tiles, all_rows, _ = keep.shape
    rows = all_rows // 2
    late = early is not None
    sums = (fields, tiles, rows, width)
    scratch = [pltpu.VMEM(sums, F32), pltpu.VMEM((tiles, 2, rows, width), BF16)]
    part = jax.ShapeDtypeStruct((tiles, rows, width), F32)
    if late:
        out_shape = [part, jax.ShapeDtypeStruct((tiles, all_rows, width), F32)]
        scratch = [pltpu.VMEM(sums, BF16)] + scratch
    else:
        out_shape = [jax.ShapeDtypeStruct(sums, BF16), part, part]
    operands = [keep, wiener, scale, matrix, response, *chunks, *(early or [])]
    return pl.pallas_call(
        functools.partial(half_kernel, splits, order, late),
        out_shape=out_shape,
        in_specs=[VMEM] * len(operands),
        out_specs=[VMEM] * len(out_shape),
        scratch_shapes=scratch,
        compiler_params=PARAMS,
        cost_estimate=cost(2 * (fields + 2) * tiles * rows * width * width, 16 * tiles * rows * width),
        name="late_half" if late else "early_half",
    )(*operands)


def slope(values):
    rows = values.shape[0]
    line = lax.broadcasted_iota(jnp.int32, values.shape, 0)
    above = jnp.where(line == rows - 1, 0.0, pltpu.roll(values, rows - 1, 0))
    below = jnp.where(line == 0, 0.0, pltpu.roll(values, 1, 0))
    return (above - below) * 0.5


def edges_kernel(splits, order, keep_ref, *refs):
    place, band = place_and_band(splits)
    sides = rim_sides(splits, band)
    weights, chunks = refs[: len(sides)], refs[len(sides) : len(sides) + splits]
    outs, (block, outermost, inner) = refs[-3 - len(sides) : -3], refs[-3:]
    fields, depth, width = chunks[0].shape
    tiles, rows, _ = keep_ref.shape
    outermost[...] = jnp.zeros_like(outermost)
    inner[...] = jnp.zeros_like(inner)
    for upper, weight_ref, out_ref in zip(sides, weights, outs):
        edge_row = jnp.where(upper, rows - depth, 0)
        there = pl.ds(pl.multiple_of(edge_row, depth), depth)
        for d, chunk in zip(order, chunks):
            half, row, tile = slot_at(place, d, tiles, depth)

            @pl.when(half * (rows // 2) + row == edge_row)
            def _():
                keep = keep_ref[tile, there, :]
                for field in range(fields):
                    block[...] = (chunk[field] * keep).astype(F32)
                    last = jnp.where(upper, depth - 1, 0)
                    outermost[field : field + 1, :] = block[pl.ds(last, 1), :]
                    inner[field : field + 1, :] = block[pl.ds(jnp.where(upper, depth - 2, 1), 1), :]
                columns = pl.ds(pl.multiple_of(tile * width, width), width)
                beyond = weight_ref[:, columns].astype(F32) * inner[...]
                outermost[fields : fields + 1, :] = jnp.sum(beyond, axis=0, keepdims=True)
                out_ref[:, columns] = outermost[...].astype(BF16)


def edges(splits, order, keep, w_edge, chunks, after):
    fields, depth, width = chunks[0].shape
    rims = rim_shapes(splits, fields, keep.shape[0] * width)
    rows = rims[0].shape[0]
    return pl.pallas_call(
        functools.partial(edges_kernel, splits, order),
        out_shape=rims,
        in_specs=[VMEM] * (splits + 1 + len(rims)) + [ANY] * len(after),
        out_specs=[VMEM] * len(rims),
        scratch_shapes=[
            pltpu.VMEM((depth, width), F32),
            pltpu.VMEM((rows, width), F32),
            pltpu.VMEM((rows, width), F32),
        ],
        compiler_params=PARAMS,
        cost_estimate=cost(0, 2 * splits * fields * depth * width),
        name="edges",
    )(keep, *w_edge, *chunks, *after)


def finish_kernel(splits, fields, early_ref, late_ref, dec_ref, *refs):
    rims, (out_ref, sums) = refs[:-2], refs[-2:]
    tiles, rows, width = dec_ref.shape
    half_rows = rows // 2
    place, band = place_and_band(splits)
    bands = lax.axis_size("sim") // splits
    half = slot_at(place, 0, tiles, rows * tiles // splits)[0]
    here = pl.ds(pl.multiple_of(half * half_rows, half_rows), half_rows)
    other = pl.ds(pl.multiple_of((1 - half) * half_rows, half_rows), half_rows)
    line = lax.broadcasted_iota(jnp.int32, (8, 1), 0)
    sides = [(band > 0, band == 0)] if bands == 2 else [(band > 0, False), (False, band < bands - 1)]
    for tile in range(tiles):
        sums[tile, here, :] = early_ref[tile]
        sums[tile, other, :] = late_ref[tile]
        sums[tile] = sums[tile] - slope(dec_ref[tile])
        columns = pl.ds(tile * width, width)
        for number, (low, high) in enumerate(sides):
            own_w, far_w, own, far = [
                ref[:, columns].astype(F32) for ref in rims[4 * number : 4 * number + 4]
            ]
            inner = 0.25 * jnp.sum(own_w * far, axis=0, keepdims=True)
            outer = jnp.sum(far_w * own, axis=0, keepdims=True) - far[fields : fields + 1]
            outer = 0.25 * outer
            first, last = sums[tile, :8, :], sums[tile, rows - 8 :, :]
            first += jnp.where((line == 0) & low, outer, 0.0)
            first -= jnp.where((line == 1) & low, inner, 0.0)
            last += jnp.where((line == 7) & high, outer, 0.0)
            last -= jnp.where((line == 6) & high, inner, 0.0)
            sums[tile, :8, :] = first
            sums[tile, rows - 8 :, :] = last
        out_ref[:, columns] = sums[tile]


def finish(splits, fields, early_part, late_part, dec, rims):
    tiles, rows, width = dec.shape
    return pl.pallas_call(
        functools.partial(finish_kernel, splits, fields),
        out_shape=pltpu.HBM((rows, tiles * width), F32),
        in_specs=[VMEM] * (3 + len(rims)),
        out_specs=VMEM,
        scratch_shapes=[pltpu.VMEM((tiles, rows, width), F32)],
        compiler_params=PARAMS,
        cost_estimate=cost(0, 12 * tiles * rows * width),
        name="finish",
    )(early_part, late_part, dec, *rims)


def distinct_kernel(
    splits, index_ref, ivf_ref, sim_ref, count_ref, distinct_ref, share_ref, chunk_ref, sems
):
    uses = index_ref.shape[0]
    place, _ = place_and_band(splits)
    wanted = region(place, EARLY[0], *ivf_ref.shape, *chunk_ref.shape[1:])
    copies = [pltpu.make_async_copy(ivf_ref.at[wanted], chunk_ref.at[0], sems.at[0])]
    copies[0].start()
    share_ref[0] = jnp.float32(1.0)
    for number in range(uses):
        distinct_ref[number] = index_ref[0]
        share_ref[number + 1] = jnp.float32(0.0)
    count = jnp.int32(0)
    for number in range(uses):
        same = [(index_ref[other] == index_ref[number]).astype(jnp.int32) for other in range(uses)]
        new = sum(same[:number], jnp.int32(0)) == 0
        times = sum(same, jnp.int32(0)).astype(F32)

        @pl.when(new)
        def _():
            distinct_ref[count] = index_ref[number]
            share_ref[count + 1] = times * (-1.0 / uses)

        count = count + new.astype(jnp.int32)
    count_ref[0] = count
    for number in range(uses):
        source = sim_ref.at[(distinct_ref[number],) + wanted]
        copy = pltpu.make_async_copy(source, chunk_ref.at[number + 1], sems.at[number + 1])
        copy.start()
        copies.append(copy)
    for copy in copies:
        copy.wait()


def distinct_fields(splits, sim_index, ivf_maps, sim_ivf, width):
    uses = sim_index.shape[0]
    rows, columns = ivf_maps.shape
    depth = rows * (columns // width) // splits
    return pl.pallas_call(
        functools.partial(distinct_kernel, splits),
        out_shape=[
            jax.ShapeDtypeStruct((1,), jnp.int32),
            jax.ShapeDtypeStruct((uses,), jnp.int32),
            jax.ShapeDtypeStruct((uses + 1,), F32),
            jax.ShapeDtypeStruct((uses + 1, depth, width), BF16),
        ],
        in_specs=[SMEM, ANY, ANY],
        out_specs=[SMEM] * 3 + [VMEM],
        scratch_shapes=[pltpu.SemaphoreType.DMA((uses + 1,))],
        compiler_params=WIDE_PARAMS,
        name="distinct",
    )(sim_index, ivf_maps, sim_ivf)


def estimate(
    sky_maps,
    ivf_maps,
    sim_sky,
    sim_ivf,
    ra_wiener,
    ra_gradient,
    pair_table,
    sim_index,
    shares,
    first_chunk,
    source_pixels,
    response,
):
    splits = pair_table.shape[0]
    axis_count = lax.axis_size("sim")
    bands = axis_count // splits
    place, band = place_and_band(splits)
    rows, columns = sky_maps.shape
    width = ra_gradient.shape[0]
    depth = rows * (columns // width) // splits

    def swap(block, d):
        pairs = [
            (g * bands + u, (g ^ d) * bands + u) for g in range(splits) for u in range(bands)
        ]
        return lax.ppermute(block, "sim", pairs)

    def exchange(blocks):
        moved = {d: swap(blocks[d], d) for d in EARLY + LATE}
        return {0: blocks[0], **moved}

    def neighbours(edge):
        if bands == 2:
            pairs = [((k + 1) % axis_count, k) if k % 2 else ((k - 1) % axis_count, k)
                     for k in range(axis_count)]
            return [edge[0], lax.ppermute(edge[0], "sim", pairs)]
        ahead = [(k, (k + 1) % axis_count) for k in range(axis_count)]
        back = [((k + 1) % axis_count, k) for k in range(axis_count)]
        below, above = lax.ppermute(edge[1], "sim", ahead), lax.ppermute(edge[0], "sim", back)
        return [edge[0], below, edge[1], above]

    rest = (0,) + EARLY[1:] + LATE
    sent = pack(splits, rest, sim_index, ivf_maps, sim_ivf, depth, width, [first_chunk])
    sent[EARLY[0]] = first_chunk
    arrived = exchange(sent)
    wiener, scale, w_edge = wiener_fields(splits, sim_index, shares, sky_maps, sim_sky, ra_wiener)
    w_rims = neighbours(w_edge)
    keep = keep_mask(source_pixels, band, rows, columns, width, [])
    weights, arrived[0] = prepare(pair_table, arrived[0])
    sums = exchange(mix(weights, arrived))
    shared = keep, wiener, scale, ra_gradient, response[:, None]
    early, late = (0,) + EARLY, LATE
    early_results = half_call(splits, early, *shared, [sums[d] for d in early], None)
    order = early + late
    edge = edges(splits, order, keep, w_edge, [sums[d] for d in order], early_results[1:2])
    s_rims = neighbours(edge)
    rims = [rim for n in range(0, len(s_rims), 2) for rim in w_rims[n : n + 2] + s_rims[n : n + 2]]
    late_part, dec = half_call(
        splits, late, *shared, [sums[d] for d in late], early_results[::2]
    )
    return finish(splits, shares.shape[0], early_results[1], late_part, dec, rims)


def on_device(
    sky_maps,
    ivf_maps,
    sim_sky,
    sim_ivf,
    ra_wiener,
    ra_gradient,
    pair_table,
    sim_index,
    source_pixels,
    response,
):
    uses = sim_index.shape[0]
    splits = pair_table.shape[0]
    width = ra_gradient.shape[0]
    count, distinct, shares, chunk = distinct_fields(splits, sim_index, ivf_maps, sim_ivf, width)
    sizes = range(max(1, uses - 2), uses + 1)

    def of_size(size):
        def run(distinct, shares, chunk):
            return estimate(
                sky_maps,
                ivf_maps,
                sim_sky,
                sim_ivf,
                ra_wiener,
                ra_gradient,
                pair_table,
                distinct[:size],
                shares[: size + 1],
                chunk[: size + 1],
                source_pixels,
                response,
            )

        return run

    branch = jnp.clip(count[0] - sizes[0], 0, len(sizes) - 1)
    return lax.switch(branch, [of_size(size) for size in sizes], distinct, shares, chunk)


def solution(mesh):
    in_specs = (
        P(("patch", "sim"), None),
        P(("patch", "sim"), None),
        P(None, ("patch", "sim"), None),
        P(None, ("patch", "sim"), None),
        P(),
        P(),
        P(),
        P(),
        P("patch"),
        P("patch"),
    )
    out_specs = P(("patch", "sim"), None)
    return jax.shard_map(
        on_device, mesh=mesh, in_specs=in_specs, out_specs=out_specs, check_vma=False
    )
```

```python
import functools

import jax
import jax.numpy as jnp
from jax import lax
from jax.experimental import pallas as pl
from jax.experimental.pallas import tpu as pltpu
from jax.sharding import PartitionSpec as P

PIXEL_CHUNK = 1024
LOW_COLUMNS = 256
MIB = 1024 * 1024

F32 = jnp.float32
BF16 = jnp.bfloat16
SMEM = pl.BlockSpec(memory_space=pltpu.SMEM)
VMEM = pl.BlockSpec(memory_space=pltpu.VMEM)
ANY = pl.BlockSpec(memory_space=pl.ANY)
WIDE_PARAMS = pltpu.CompilerParams(vmem_limit_bytes=60 * MIB)
PARAMS = pltpu.CompilerParams(vmem_limit_bytes=24 * MIB)

EARLY = (6, 1, 7)
LATE = (2, 3, 5, 4)


def cost(flops, bytes_accessed):
    return pl.CostEstimate(flops=int(flops), bytes_accessed=int(bytes_accessed), transcendentals=0)


def place_and_band(splits):
    count = lax.axis_size("sim")
    bands = count // splits
    device = lax.axis_index("sim")
    logical = lax.rem(device + (count - bands // 2), count)
    return lax.div(device, bands), lax.rem(logical, bands)


def slot_at(place, d, tiles, depth):
    slot = lax.bitwise_xor(place, d)
    block = lax.div(slot, tiles)
    half = lax.bitwise_and(lax.bitwise_xor(block, lax.div(block, 2)), 1)
    return half, pl.multiple_of(lax.div(block, 2) * depth, depth), lax.rem(slot, tiles)


def keep_kernel(rows, width, a_ref, b_ref, *refs):
    keep_ref, total = refs[-2:]
    pixels = a_ref.shape[1]
    tall = total.shape[0]
    total[...] = jnp.zeros_like(total)

    @pl.loop(0, pixels // PIXEL_CHUNK)
    def _(step):
        part = pl.ds(pl.multiple_of(step * PIXEL_CHUNK, PIXEL_CHUNK), PIXEL_CHUNK)
        high = lax.broadcasted_iota(jnp.int32, (tall, PIXEL_CHUNK), 0) == a_ref[:, part]
        low = lax.broadcasted_iota(jnp.int32, (LOW_COLUMNS, PIXEL_CHUNK), 0) == b_ref[:, part]
        total[...] += lax.dot_general(
            high.astype(F32).astype(BF16),
            low.astype(F32).astype(BF16),
            (((1,), (1,)), ((), ())),
            preferred_element_type=F32,
        )

    per_tile = width // LOW_COLUMNS
    for block in range(tall // rows):
        tile, piece = block // per_tile, block % per_tile
        count = total[block * rows : (block + 1) * rows, :]
        keep_ref[tile, :, piece * LOW_COLUMNS : (piece + 1) * LOW_COLUMNS] = jnp.where(
            count > 0, 0.0, 1.0
        ).astype(BF16)


def keep_mask(source_pixels, band_index, rows, columns, width, after):
    offsets = source_pixels - band_index * rows * columns
    inside = (offsets >= 0) & (offsets < rows * columns)
    row, column = offsets // columns, offsets % columns
    a = jnp.where(inside, (column // LOW_COLUMNS) * rows + row, -1)
    b = column % LOW_COLUMNS
    pixels = source_pixels.shape[0]
    extra = -pixels % PIXEL_CHUNK
    a = jnp.pad(a, (0, extra), constant_values=-1)[None]
    b = jnp.pad(b, (0, extra))[None]
    tall = columns // LOW_COLUMNS * rows
    return pl.pallas_call(
        functools.partial(keep_kernel, rows, width),
        out_shape=jax.ShapeDtypeStruct((columns // width, rows, width), BF16),
        in_specs=[VMEM, VMEM] + [ANY] * len(after),
        out_specs=VMEM,
        scratch_shapes=[pltpu.VMEM((tall, LOW_COLUMNS), F32)],
        compiler_params=PARAMS,
        cost_estimate=cost(2 * tall * LOW_COLUMNS * (pixels + extra), 4 * rows * columns),
        name="keep",
    )(a, b, *after)


def rim_sides(splits, band):
    if lax.axis_size("sim") // splits == 2:
        return [band == 0]
    return [False, True]


def as_rows(values, rows, width):
    values = values + [jnp.zeros((rows - len(values), width), F32)]
    return jnp.concatenate(values, axis=0).astype(BF16)


def wiener_kernel(splits, index_ref, share_ref, sky_ref, sim_ref, matrix_ref, out_ref, *refs):
    scale_ref, edge_refs, (held, sems) = refs[0], refs[1:-2], refs[-2:]
    fields, tiles, rows, width = out_ref.shape
    copies = [pltpu.make_async_copy(sky_ref, held.at[0], sems.at[0])]
    for field in range(1, fields):
        source = sim_ref.at[index_ref[field - 1]]
        copies.append(pltpu.make_async_copy(source, held.at[field], sems.at[field]))
    for copy in copies:
        copy.start()
    for copy in copies:
        copy.wait()
    for tile in range(tiles):
        values = held[:, :, tile * width : (tile + 1) * width].reshape(fields * rows, width)
        result = jnp.dot(values, matrix_ref[...], preferred_element_type=F32).astype(BF16)
        out_ref[:, tile] = result.reshape(fields, rows, width)
    for field in range(fields):
        scale_ref[field : field + 1, :] = jnp.full((1, scale_ref.shape[1]), share_ref[field], F32)
    _, band = place_and_band(splits)
    for upper, edge_ref in zip(rim_sides(splits, band), edge_refs):
        for tile in range(tiles):
            picked = []
            for field in range(fields):
                low = out_ref[field, tile, :16, :].astype(F32)[:1]
                high = out_ref[field, tile, rows - 16 :, :].astype(F32)[15:]
                picked.append(jnp.where(upper, high, low) * share_ref[field])
            columns = pl.ds(tile * width, width)
            edge_ref[:, columns] = as_rows(picked, edge_ref.shape[0], width)


def rim_shapes(splits, fields, columns):
    count = 1 if lax.axis_size("sim") // splits == 2 else 2
    return [jax.ShapeDtypeStruct((-(-(fields + 1) // 8) * 8, columns), BF16)] * count


def wiener_fields(splits, sim_index, shares, sky_maps, sim_sky, matrix):
    rows, columns = sky_maps.shape
    width = matrix.shape[0]
    fields = sim_index.shape[0] + 1
    rims = rim_shapes(splits, fields, columns)
    wiener, scale, *edge = pl.pallas_call(
        functools.partial(wiener_kernel, splits),
        out_shape=[
            jax.ShapeDtypeStruct((fields, columns // width, rows, width), BF16),
            jax.ShapeDtypeStruct((-(-fields // 8) * 8, 128), F32),
            *rims,
        ],
        in_specs=[SMEM, SMEM, ANY, ANY, VMEM],
        out_specs=[VMEM] * (2 + len(rims)),
        scratch_shapes=[
            pltpu.VMEM((fields, rows, columns), BF16),
            pltpu.SemaphoreType.DMA((fields,)),
        ],
        compiler_params=PARAMS,
        cost_estimate=cost(2 * fields * rows * columns * width, 4 * fields * rows * columns),
        name="wiener",
    )(sim_index, shares, sky_maps, sim_sky, matrix)
    return wiener, scale, edge


def region(place, d, rows, columns, depth, width):
    half, row, tile = slot_at(place, d, columns // width, depth)
    part = pl.ds(pl.multiple_of(half * (rows // 2) + row, depth), depth)
    return part, pl.ds(pl.multiple_of(tile * width, width), width)


def pack_kernel(splits, order, index_ref, ivf_ref, sim_ref, *refs):
    outs, held, sems = refs[-2 - len(order) : -2], refs[-2], refs[-1]
    fields, depth, width = outs[0].shape
    rows, columns = ivf_ref.shape
    place, _ = place_and_band(splits)
    copies = [pltpu.make_async_copy(ivf_ref, held.at[0], sems.at[0])]
    for field in range(1, fields):
        source = sim_ref.at[index_ref[field - 1]]
        copies.append(pltpu.make_async_copy(source, held.at[field], sems.at[field]))
    for copy in copies:
        copy.start()
    for field in range(fields):
        copies[field].wait()
        for d, out in zip(order, outs):
            out[field] = held[(field,) + region(place, d, rows, columns, depth, width)]


def pack(splits, order, sim_index, ivf_maps, sim_ivf, depth, width, after):
    fields = sim_index.shape[0] + 1
    chunks = pl.pallas_call(
        functools.partial(pack_kernel, splits, order),
        out_shape=[jax.ShapeDtypeStruct((fields, depth, width), BF16)] * len(order),
        in_specs=[SMEM, ANY, ANY] + [ANY] * len(after),
        out_specs=[VMEM] * len(order),
        scratch_shapes=[
            pltpu.VMEM((fields,) + ivf_maps.shape, BF16),
            pltpu.SemaphoreType.DMA((fields,)),
        ],
        compiler_params=WIDE_PARAMS,
        cost_estimate=cost(0, 4 * len(order) * fields * depth * width),
        name="pack",
    )(sim_index, ivf_maps, sim_ivf, *after)
    return dict(zip(order, chunks))


def prepare_kernel(splits, pair_ref, own_ref, weights_ref, held_ref, sem):
    copy = pltpu.make_async_copy(own_ref, held_ref, sem)
    copy.start()
    size = weights_ref.shape[0]
    depth = size // splits
    place, band = place_and_band(splits)
    bands = lax.axis_size("sim") // splits
    shift = (band >= bands - bands // 2).astype(jnp.int32)
    split_of = [lax.rem(lax.bitwise_xor(place, d) + splits - shift, splits) for d in range(splits)]
    row = lax.broadcasted_iota(jnp.int32, (size, size), 0)
    column = lax.broadcasted_iota(jnp.int32, (size, size), 1)
    total = jnp.zeros((size, size), F32)
    for d in range(splits):
        for e in range(splits):
            if d != e:
                here = (lax.div(row, depth) == d) & (lax.div(column, depth) == e)
                value = pair_ref[split_of[d], split_of[e]].astype(F32)
                total = jnp.where(here, value, total)
    same = lax.rem(row, depth) == lax.rem(column, depth)
    weights_ref[...] = jnp.where(same, total, 0.0).astype(BF16)
    copy.wait()


def prepare(pair_table, own):
    splits = pair_table.shape[0]
    size = splits * own.shape[1]
    return pl.pallas_call(
        functools.partial(prepare_kernel, splits),
        out_shape=[
            jax.ShapeDtypeStruct((size, size), BF16),
            jax.ShapeDtypeStruct(own.shape, BF16),
        ],
        in_specs=[SMEM, ANY],
        out_specs=[VMEM, VMEM],
        scratch_shapes=[pltpu.SemaphoreType.DMA],
        compiler_params=PARAMS,
        cost_estimate=cost(splits * splits * size * size, 4 * own.size),
        name="prepare",
    )(pair_table, own)


def mix_kernel(order, weights_ref, *refs):
    parts = len(order)
    chunks, outs = refs[:parts], refs[parts:]
    fields, depth, _ = chunks[0].shape
    for field in range(fields):
        stacked = jnp.concatenate([chunks[order.index(d)][field] for d in range(parts)], axis=0)
        mixed = jnp.dot(weights_ref[...], stacked, preferred_element_type=F32).astype(BF16)
        for d in range(parts):
            outs[d][field] = mixed[d * depth : (d + 1) * depth]


def mix(weights, chunks):
    order = EARLY + LATE + (0,)
    parts = len(chunks)
    shape = chunks[0].shape
    size = shape[0] * shape[1] * shape[2]
    return pl.pallas_call(
        functools.partial(mix_kernel, order),
        out_shape=[jax.ShapeDtypeStruct(shape, BF16)] * parts,
        in_specs=[VMEM] * (parts + 1),
        out_specs=[VMEM] * parts,
        compiler_params=PARAMS,
        cost_estimate=cost(2 * parts * size * weights.shape[0], 4 * parts * size),
        name="mix",
    )(weights, *[chunks[d] for d in order])


def half_kernel(
    splits, order, late, keep_ref, wiener_ref, scale_ref, matrix_ref, response_ref, *refs
):
    chunks = refs[: len(order)]
    fields, depth, width = chunks[0].shape
    if late:
        early_sums_ref, early_dec_ref = refs[len(order) : len(order) + 2]
        part_ref, dec_ref, sums_ref, grad_ref, ra_ref = refs[len(order) + 2 :]
    else:
        sums_ref, part_ref, early_dec_ref, grad_ref, ra_ref = refs[len(order) :]
    tiles, rows = sums_ref.shape[1:3]
    place, band = place_and_band(splits)
    half = slot_at(place, order[0], tiles, depth)[0]
    here = pl.ds(pl.multiple_of(half * rows, rows), rows)
    other = pl.ds(pl.multiple_of((1 - half) * rows, rows), rows)
    for d, chunk in zip(order, chunks):
        _, row, tile = slot_at(place, d, tiles, depth)
        there = pl.ds(pl.multiple_of(half * rows + row, depth), depth)
        keep = keep_ref[tile, there, :]
        for field in range(fields):
            sums_ref[field, tile, pl.ds(row, depth), :] = chunk[field] * keep
    grad_ref[...] = jnp.dot(
        sums_ref[...].reshape(fields * tiles * rows, width),
        matrix_ref[...],
        preferred_element_type=F32,
    ).reshape(grad_ref.shape)
    response = response_ref[pl.ds(pl.multiple_of((2 * band + half) * rows, rows), rows), :]
    line = lax.broadcasted_iota(jnp.int32, (rows, width), 0)
    sources = []
    for tile in range(tiles):
        ra = dec = src = first = last = 0.0
        for field in range(fields):
            wide = sums_ref[field, tile].astype(F32)
            share = scale_ref[field : field + 1, :1]
            weight = wiener_ref[field, tile, here, :].astype(F32) * share
            above, below = pltpu.roll(wide, rows - 1, 0), pltpu.roll(wide, 1, 0)
            above_fill = below_fill = 0.0
            if late:
                near = early_sums_ref[field, tile].astype(F32)
                above_fill = jnp.where(half == 0, near[:1], 0.0)
                below_fill = jnp.where(half == 1, near[rows - 1 :], 0.0)
                beside = wiener_ref[field, tile, other, :].astype(F32) * share
                last = last + 0.5 * beside[rows - 1 :] * wide[:1]
                first = first - 0.5 * beside[:1] * wide[rows - 1 :]
            above = jnp.where(line == rows - 1, above_fill, above)
            below = jnp.where(line == 0, below_fill, below)
            ra = ra + weight * grad_ref[field, tile]
            dec = dec + weight * ((above - below) * 0.5)
            src = src + weight * wide
        high = ra.astype(BF16)
        ra_ref[tile, 0] = high
        ra_ref[tile, 1] = (ra - high.astype(F32)).astype(BF16)
        sources.append(response * src)
        if late:
            early_dec = early_dec_ref[tile]
            early_dec = early_dec + jnp.where((line == rows - 1) & (half == 1), last, 0.0)
            early_dec = early_dec + jnp.where((line == 0) & (half == 0), first, 0.0)
            dec_ref[tile, here, :] = dec
            dec_ref[tile, other, :] = early_dec
        else:
            early_dec_ref[tile] = dec
    both = jnp.dot(
        ra_ref[...].reshape(tiles * 2 * rows, width), matrix_ref[...], preferred_element_type=F32
    ).reshape(tiles, 2, rows, width)
    for tile in range(tiles):
        part_ref[tile] = -(both[tile, 0] + both[tile, 1]) - sources[tile]


def half_call(splits, order, keep, wiener, scale, matrix, response, chunks, early):
    fields, depth, width = chunks[0].shape
    tiles, all_rows, _ = keep.shape
    rows = all_rows // 2
    late = early is not None
    sums = (fields, tiles, rows, width)
    scratch = [pltpu.VMEM(sums, F32), pltpu.VMEM((tiles, 2, rows, width), BF16)]
    part = jax.ShapeDtypeStruct((tiles, rows, width), F32)
    if late:
        out_shape = [part, jax.ShapeDtypeStruct((tiles, all_rows, width), F32)]
        scratch = [pltpu.VMEM(sums, BF16)] + scratch
    else:
        out_shape = [jax.ShapeDtypeStruct(sums, BF16), part, part]
    operands = [keep, wiener, scale, matrix, response, *chunks, *(early or [])]
    return pl.pallas_call(
        functools.partial(half_kernel, splits, order, late),
        out_shape=out_shape,
        in_specs=[VMEM] * len(operands),
        out_specs=[VMEM] * len(out_shape),
        scratch_shapes=scratch,
        compiler_params=PARAMS,
        cost_estimate=cost(2 * (fields + 2) * tiles * rows * width * width, 16 * tiles * rows * width),
        name="late_half" if late else "early_half",
    )(*operands)


def slope(values):
    rows = values.shape[0]
    line = lax.broadcasted_iota(jnp.int32, values.shape, 0)
    above = jnp.where(line == rows - 1, 0.0, pltpu.roll(values, rows - 1, 0))
    below = jnp.where(line == 0, 0.0, pltpu.roll(values, 1, 0))
    return (above - below) * 0.5


def edges_kernel(splits, order, keep_ref, *refs):
    place, band = place_and_band(splits)
    sides = rim_sides(splits, band)
    weights, chunks = refs[: len(sides)], refs[len(sides) : len(sides) + splits]
    outs, (block, outermost, inner) = refs[-3 - len(sides) : -3], refs[-3:]
    fields, depth, width = chunks[0].shape
    tiles, rows, _ = keep_ref.shape
    outermost[...] = jnp.zeros_like(outermost)
    inner[...] = jnp.zeros_like(inner)
    for upper, weight_ref, out_ref in zip(sides, weights, outs):
        edge_row = jnp.where(upper, rows - depth, 0)
        there = pl.ds(pl.multiple_of(edge_row, depth), depth)
        for d, chunk in zip(order, chunks):
            half, row, tile = slot_at(place, d, tiles, depth)

            @pl.when(half * (rows // 2) + row == edge_row)
            def _():
                keep = keep_ref[tile, there, :]
                for field in range(fields):
                    block[...] = (chunk[field] * keep).astype(F32)
                    last = jnp.where(upper, depth - 1, 0)
                    outermost[field : field + 1, :] = block[pl.ds(last, 1), :]
                    inner[field : field + 1, :] = block[pl.ds(jnp.where(upper, depth - 2, 1), 1), :]
                columns = pl.ds(pl.multiple_of(tile * width, width), width)
                beyond = weight_ref[:, columns].astype(F32) * inner[...]
                outermost[fields : fields + 1, :] = jnp.sum(beyond, axis=0, keepdims=True)
                out_ref[:, columns] = outermost[...].astype(BF16)


def edges(splits, order, keep, w_edge, chunks, after):
    fields, depth, width = chunks[0].shape
    rims = rim_shapes(splits, fields, keep.shape[0] * width)
    rows = rims[0].shape[0]
    return pl.pallas_call(
        functools.partial(edges_kernel, splits, order),
        out_shape=rims,
        in_specs=[VMEM] * (splits + 1 + len(rims)) + [ANY] * len(after),
        out_specs=[VMEM] * len(rims),
        scratch_shapes=[
            pltpu.VMEM((depth, width), F32),
            pltpu.VMEM((rows, width), F32),
            pltpu.VMEM((rows, width), F32),
        ],
        compiler_params=PARAMS,
        cost_estimate=cost(0, 2 * splits * fields * depth * width),
        name="edges",
    )(keep, *w_edge, *chunks, *after)


def finish_kernel(splits, fields, early_ref, late_ref, dec_ref, *refs):
    rims, (out_ref, sums, sems) = refs[:-3], refs[-3:]
    tiles, rows, width = dec_ref.shape
    half_rows = rows // 2
    place, band = place_and_band(splits)
    bands = lax.axis_size("sim") // splits
    half = slot_at(place, 0, tiles, rows * tiles // splits)[0]
    here = pl.ds(pl.multiple_of(half * half_rows, half_rows), half_rows)
    other = pl.ds(pl.multiple_of((1 - half) * half_rows, half_rows), half_rows)
    line = lax.broadcasted_iota(jnp.int32, (8, 1), 0)
    sides = [(band > 0, band == 0)] if bands == 2 else [(band > 0, False), (False, band < bands - 1)]
    copies = []
    for tile in range(tiles):
        sums[tile, here, :] = early_ref[tile]
        sums[tile, other, :] = late_ref[tile]
        sums[tile] = sums[tile] - slope(dec_ref[tile])
        columns = pl.ds(tile * width, width)
        for number, (low, high) in enumerate(sides):
            own_w, far_w, own, far = [
                ref[:, columns].astype(F32) for ref in rims[4 * number : 4 * number + 4]
            ]
            inner = 0.25 * jnp.sum(own_w * far, axis=0, keepdims=True)
            outer = jnp.sum(far_w * own, axis=0, keepdims=True) - far[fields : fields + 1]
            outer = 0.25 * outer
            first, last = sums[tile, :8, :], sums[tile, rows - 8 :, :]
            first += jnp.where((line == 0) & low, outer, 0.0)
            first -= jnp.where((line == 1) & low, inner, 0.0)
            last += jnp.where((line == 7) & high, outer, 0.0)
            last -= jnp.where((line == 6) & high, inner, 0.0)
            sums[tile, :8, :] = first
            sums[tile, rows - 8 :, :] = last
        copy = pltpu.make_async_copy(sums.at[tile], out_ref.at[:, columns], sems.at[tile])
        copy.start()
        copies.append(copy)
    for copy in copies:
        copy.wait()


def finish(splits, fields, early_part, late_part, dec, rims):
    tiles, rows, width = dec.shape
    return pl.pallas_call(
        functools.partial(finish_kernel, splits, fields),
        out_shape=pltpu.HBM((rows, tiles * width), F32),
        in_specs=[VMEM] * (3 + len(rims)),
        out_specs=pl.BlockSpec(memory_space=pltpu.HBM),
        scratch_shapes=[
            pltpu.VMEM((tiles, rows, width), F32),
            pltpu.SemaphoreType.DMA((tiles,)),
        ],
        compiler_params=PARAMS,
        cost_estimate=cost(0, 12 * tiles * rows * width),
        name="finish",
    )(early_part, late_part, dec, *rims)


def distinct_kernel(
    splits, index_ref, ivf_ref, sim_ref, count_ref, distinct_ref, share_ref, chunk_ref, sems
):
    uses = index_ref.shape[0]
    place, _ = place_and_band(splits)
    wanted = region(place, EARLY[0], *ivf_ref.shape, *chunk_ref.shape[1:])
    copies = [pltpu.make_async_copy(ivf_ref.at[wanted], chunk_ref.at[0], sems.at[0])]
    copies[0].start()
    share_ref[0] = jnp.float32(1.0)
    for number in range(uses):
        distinct_ref[number] = index_ref[0]
        share_ref[number + 1] = jnp.float32(0.0)
    count = jnp.int32(0)
    for number in range(uses):
        same = [(index_ref[other] == index_ref[number]).astype(jnp.int32) for other in range(uses)]
        new = sum(same[:number], jnp.int32(0)) == 0
        times = sum(same, jnp.int32(0)).astype(F32)

        @pl.when(new)
        def _():
            distinct_ref[count] = index_ref[number]
            share_ref[count + 1] = times * (-1.0 / uses)

        count = count + new.astype(jnp.int32)
    count_ref[0] = count
    for number in range(uses):
        source = sim_ref.at[(distinct_ref[number],) + wanted]
        copy = pltpu.make_async_copy(source, chunk_ref.at[number + 1], sems.at[number + 1])
        copy.start()
        copies.append(copy)
    for copy in copies:
        copy.wait()


def distinct_fields(splits, sim_index, ivf_maps, sim_ivf, width):
    uses = sim_index.shape[0]
    rows, columns = ivf_maps.shape
    depth = rows * (columns // width) // splits
    return pl.pallas_call(
        functools.partial(distinct_kernel, splits),
        out_shape=[
            jax.ShapeDtypeStruct((1,), jnp.int32),
            jax.ShapeDtypeStruct((uses,), jnp.int32),
            jax.ShapeDtypeStruct((uses + 1,), F32),
            jax.ShapeDtypeStruct((uses + 1, depth, width), BF16),
        ],
        in_specs=[SMEM, ANY, ANY],
        out_specs=[SMEM] * 3 + [VMEM],
        scratch_shapes=[pltpu.SemaphoreType.DMA((uses + 1,))],
        compiler_params=WIDE_PARAMS,
        name="distinct",
    )(sim_index, ivf_maps, sim_ivf)


def estimate(
    sky_maps,
    ivf_maps,
    sim_sky,
    sim_ivf,
    ra_wiener,
    ra_gradient,
    pair_table,
    sim_index,
    shares,
    first_chunk,
    source_pixels,
    response,
):
    splits = pair_table.shape[0]
    axis_count = lax.axis_size("sim")
    bands = axis_count // splits
    place, band = place_and_band(splits)
    rows, columns = sky_maps.shape
    width = ra_gradient.shape[0]
    depth = rows * (columns // width) // splits

    def swap(block, d):
        pairs = [
            (g * bands + u, (g ^ d) * bands + u) for g in range(splits) for u in range(bands)
        ]
        return lax.ppermute(block, "sim", pairs)

    def exchange(blocks):
        moved = {d: swap(blocks[d], d) for d in EARLY + LATE}
        return {0: blocks[0], **moved}

    def neighbours(edge):
        if bands == 2:
            pairs = [((k + 1) % axis_count, k) if k % 2 else ((k - 1) % axis_count, k)
                     for k in range(axis_count)]
            return [edge[0], lax.ppermute(edge[0], "sim", pairs)]
        ahead = [(k, (k + 1) % axis_count) for k in range(axis_count)]
        back = [((k + 1) % axis_count, k) for k in range(axis_count)]
        below, above = lax.ppermute(edge[1], "sim", ahead), lax.ppermute(edge[0], "sim", back)
        return [edge[0], below, edge[1], above]

    rest = (0,) + EARLY[1:] + LATE
    sent = pack(splits, rest, sim_index, ivf_maps, sim_ivf, depth, width, [first_chunk])
    sent[EARLY[0]] = first_chunk
    arrived = exchange(sent)
    wiener, scale, w_edge = wiener_fields(splits, sim_index, shares, sky_maps, sim_sky, ra_wiener)
    w_rims = neighbours(w_edge)
    keep = keep_mask(source_pixels, band, rows, columns, width, [])
    weights, arrived[0] = prepare(pair_table, arrived[0])
    sums = exchange(mix(weights, arrived))
    shared = keep, wiener, scale, ra_gradient, response[:, None]
    early, late = (0,) + EARLY, LATE
    early_results = half_call(splits, early, *shared, [sums[d] for d in early], None)
    order = early + late
    edge = edges(splits, order, keep, w_edge, [sums[d] for d in order], early_results[1:2])
    s_rims = neighbours(edge)
    rims = [rim for n in range(0, len(s_rims), 2) for rim in w_rims[n : n + 2] + s_rims[n : n + 2]]
    late_part, dec = half_call(
        splits, late, *shared, [sums[d] for d in late], early_results[::2]
    )
    return finish(splits, shares.shape[0], early_results[1], late_part, dec, rims)


def on_device(
    sky_maps,
    ivf_maps,
    sim_sky,
    sim_ivf,
    ra_wiener,
    ra_gradient,
    pair_table,
    sim_index,
    source_pixels,
    response,
):
    uses = sim_index.shape[0]
    splits = pair_table.shape[0]
    width = ra_gradient.shape[0]
    count, distinct, shares, chunk = distinct_fields(splits, sim_index, ivf_maps, sim_ivf, width)
    sizes = range(max(1, uses - 2), uses + 1)

    def of_size(size):
        def run(distinct, shares, chunk):
            return estimate(
                sky_maps,
                ivf_maps,
                sim_sky,
                sim_ivf,
                ra_wiener,
                ra_gradient,
                pair_table,
                distinct[:size],
                shares[: size + 1],
                chunk[: size + 1],
                source_pixels,
                response,
            )

        return run

    branch = jnp.clip(count[0] - sizes[0], 0, len(sizes) - 1)
    return lax.switch(branch, [of_size(size) for size in sizes], distinct, shares, chunk)


def solution(mesh):
    in_specs = (
        P(("patch", "sim"), None),
        P(("patch", "sim"), None),
        P(None, ("patch", "sim"), None),
        P(None, ("patch", "sim"), None),
        P(),
        P(),
        P(),
        P(),
        P("patch"),
        P("patch"),
    )
    out_specs = P(("patch", "sim"), None)
    return jax.shard_map(
        on_device, mesh=mesh, in_specs=in_specs, out_specs=out_specs, check_vma=False
    )
```
